512 devices in a mesh: client: 32 (over x, y, core), shard: 16 (over z).
Axes of the slice: x: 4, y: 4, z: 16, core: 2. Of those that a mesh axis runs over, the one named last changes fastest.
Arguments:
- updates: bfloat16 [384, 192, 14336], P('client', 'shard'), may hold values from -2000 to 2000
- momentum: float32 [192, 14336], P('shard', 'client'), may hold values from -6 to 6
- log_thresholds: float32 [12], replicated, may hold values from 0 to 20
- cohort_of: int32 [384], replicated, may hold values from 0 to 11, as said below
- seeds: int32 [8], replicated, may hold values from 0 to 1073741823
- round_index: int32 [1], replicated, may hold values from 8 to 99999
- coef_index: int32 [1], replicated, may hold values from 0 to 7
Outputs:
- momentum_next: float32 [192, 14336], P('shard', 'client')
- log_next: float32 [12], replicated
The draws below stay inside these ranges and needn't reach their ends.
Inputs may be any that keep to these rules, and one draw needn't show every extreme that they name: `cohort_of`: each of the 12 cohorts is named by exactly 32 clients.
All inputs are finite; a program needn't handle non-finite values.
Results may differ from the reference program's by a relative error of at most 0.0003.
Values sent between devices are 32-bit elements; how exact they have to be, the bound alone decides.
No kernel may reach another device: no remote copies, remote signals or barrier semaphores. Data moves between devices by JAX's collectives and lax.ppermute only.
A program may use at most 64 MiB of HBM per device.

```python
import math
import jax
import jax.numpy as jnp
from jax import lax

FF = 14336
BAND = 8
COHORTS = 12
ROWS = 192
CLIENTS = 384


def cohort_table(key):
    order = jax.random.permutation(jax.random.fold_in(key, 101), CLIENTS)
    return (order // (CLIENTS // COHORTS)).astype(jnp.int32)


def threshold_table(key, spread):
    base = 0.5 * jnp.log(jnp.float32(ROWS * FF))
    return base + spread * jax.random.uniform(jax.random.fold_in(key, 102), (COHORTS,), jnp.float32)


def draw_cohort_of(key, part):
    table = cohort_table(key)
    return table


def draw_log_thresholds(key, part):
    spread = 1.5
    table = threshold_table(key, spread)
    return table


def draw_updates(key, part):
    spread = 1.5
    log_limit = threshold_table(key, spread)
    cohort = cohort_table(key)
    key = jax.random.fold_in(key, 5)
    keys = jax.random.split(key, 7)
    common = jax.random.normal(keys[0], (ROWS, FF), jnp.float32)
    row_scale = jnp.exp(jax.random.uniform(keys[1], (ROWS,), jnp.float32, 0.0, 0.5 * math.log(10.0)))
    col_scale = jnp.exp(jax.random.uniform(keys[2], (FF,), jnp.float32, 0.0, 0.5 * math.log(10.0)))
    mass = jnp.sum(row_scale * row_scale) * jnp.sum(col_scale * col_scale)
    ratio = jnp.exp(jax.random.uniform(keys[4], (CLIENTS,), jnp.float32, math.log(0.7), math.log(1.4)))
    scale = jnp.exp(log_limit)[cohort] * ratio / jnp.sqrt(mass)
    outer = row_scale[:, None] * col_scale[None, :]
    own = jax.random.normal(keys[6], (CLIENTS, ROWS, FF), jnp.float32)
    return (scale[:, None, None] * outer[None] * (0.6 * common[None] + 0.8 * own)).astype(jnp.bfloat16)


def place_ends(drawn, stream_key, low, high):
    extent = drawn.shape
    spot = [jax.random.randint(jax.random.fold_in(stream_key, axis), (), 0, extent[axis]) for axis in range(len(extent))]
    drawn = drawn.at[tuple(spot)].set(low)
    longest = extent.index(max(extent))
    spot[longest] = (spot[longest] + 1) % extent[longest]
    return drawn.at[tuple(spot)].set(high)


def levels(own_key, shape, cuts, low, largest):
    level, own = 1.0, jax.random.fold_in(own_key, 6)
    for dim, parts in cuts:
        draws = jnp.exp(jax.random.uniform(jax.random.fold_in(own, dim), (parts,), jnp.float32, low / len(cuts), largest / len(cuts)))
        level = level * jnp.repeat(draws, shape[dim] // parts).reshape([-1 if axis == dim else 1 for axis in range(len(shape))])
    return level


def scatter_about(stream_key, shape, scale, bound, cuts=(), held_as=jnp.bfloat16):
    values = scale * jax.random.normal(stream_key, shape, jnp.float32)
    if cuts:
        values = values * levels(stream_key, shape, cuts, -0.22, 0.18)
    return jnp.clip(values, -bound, bound).astype(held_as)


def setup_inputs(seed: int = 0) -> dict:
    arg_keys = jax.random.split(jax.random.key(seed), 8)
    updates = draw_updates(jax.random.fold_in(arg_keys[7], 71), 0)
    momentum = scatter_about(arg_keys[1], (ROWS, FF), 1.0, 6.0, ((0, 16), (1, 32)), jnp.float32)
    log_thresholds = draw_log_thresholds(jax.random.fold_in(arg_keys[7], 71), 0)
    cohort_of = draw_cohort_of(jax.random.fold_in(arg_keys[7], 71), 0)
    seeds = place_ends(jax.random.randint(arg_keys[4], (BAND,), 0, 1073741824), jax.random.fold_in(arg_keys[4], 1), 0, 1073741823).astype(jnp.int32)
    round_index = jax.random.randint(arg_keys[5], (1,), BAND, 100000).astype(jnp.int32)
    coef_index = jax.random.randint(arg_keys[6], (1,), 0, 8).astype(jnp.int32)
    return {"updates": updates, "momentum": momentum, "log_thresholds": log_thresholds, "cohort_of": cohort_of, "seeds": seeds, "round_index": round_index, "coef_index": coef_index}


def mix(x):
    x = x ^ lax.shift_right_logical(x, jnp.int32(16))
    x = x * jnp.int32(2146121005)
    x = x ^ lax.shift_right_logical(x, jnp.int32(15))
    x = x * jnp.int32(-2073450869)
    x = x ^ lax.shift_right_logical(x, jnp.int32(16))
    return x

def band_noise(index, seeds, round_index, coef_index):
    lags = jnp.arange(seeds.shape[0], dtype=jnp.int32)
    keys = mix(seeds ^ (round_index[0] - lags) * jnp.int32(1640531527))
    hashed = mix(index[None] * jnp.int32(1013904223) + keys[:, None, None])
    uniform = (lax.shift_right_logical(hashed, jnp.int32(8)).astype(jnp.float32) + 0.5) * (1.0 / 16777216.0)
    normal_like = 3.4641016151377544 * (uniform - 0.5)
    rate = 0.4 + 0.07 * coef_index[0].astype(jnp.float32)
    lagf = lags.astype(jnp.float32)
    ratio = jnp.where(lags == 0, 1.0, rate * (2.0 * lagf - 1.0) / (2.0 * jnp.maximum(lagf, 1.0)))
    coefs = jnp.cumprod(ratio).astype(jnp.float32)
    return lax.optimization_barrier(jnp.sum(coefs[:, None, None] * normal_like, axis=0))

def reference(updates, momentum, log_thresholds, cohort_of, seeds, round_index, coef_index):
    limits = jnp.exp(log_thresholds)

    def norm_one(update):
        return jnp.sqrt(jnp.sum(jnp.square(update.astype(jnp.float32))))
    norms = lax.map(norm_one, updates)
    client_limit = limits[cohort_of]
    factor = client_limit / jnp.maximum(norms, client_limit)
    unclipped = (norms <= client_limit).astype(jnp.float32)
    member = (cohort_of[:, None] == jnp.arange(COHORTS, dtype=jnp.int32)[None, :]).astype(jnp.float32)
    counts = lax.optimization_barrier(jnp.sum(member * unclipped[:, None], axis=0))

    def add_client(total, pair):
        weight, update = pair
        return (total + weight * update.astype(jnp.float32), None)
    clipped_sum, _ = lax.scan(add_client, jnp.zeros((ROWS, FF), jnp.float32), (factor, updates))
    row_ids = jnp.arange(ROWS, dtype=jnp.int32)
    col_ids = jnp.arange(FF, dtype=jnp.int32)
    index = row_ids[:, None] * jnp.int32(FF) + col_ids[None, :]
    noise = band_noise(index, seeds, round_index, coef_index)
    aggregate = (clipped_sum + 0.05 * jnp.max(limits) * noise) / CLIENTS
    momentum_next = 0.9 * momentum + aggregate
    log_next = log_thresholds - 0.2 * (counts / (CLIENTS // COHORTS) - 0.5)
    return (momentum_next, log_next)
```

```python
import jax
import jax.numpy as jnp
from jax import lax
from jax.experimental import pallas as pl
from jax.experimental.pallas import tpu as pltpu
from jax.sharding import PartitionSpec as P

LANES = 128
MIB = 1024 * 1024


def mix(x):
    x = x ^ lax.shift_right_logical(x, jnp.int32(16))
    x = x * jnp.int32(2146121005)
    x = x ^ lax.shift_right_logical(x, jnp.int32(15))
    x = x * jnp.int32(-2073450869)
    x = x ^ lax.shift_right_logical(x, jnp.int32(16))
    return x


def lane_ids(shape):
    return lax.broadcasted_iota(jnp.int32, shape, len(shape) - 1)


def diagonal(size):
    return lax.broadcasted_iota(jnp.int32, (size, LANES), 0) == lane_ids((size, LANES))


EVEN = (0, 1, 2, 3)
ODD = (4, 5, 6, 3)
GROUPS = 7
SLAB = 6 * LANES
HALF = LANES // 2


def fold(x):
    parts = [x[:, at : at + LANES] for at in range(0, x.shape[1], LANES)]
    while len(parts) > 1:
        parts = [sum(parts[at : at + 2]) for at in range(0, len(parts), 2)]
    return parts[0]


def square_kernel(width, round_s, coef_s, log_hbm, cohort_hbm, seeds_hbm, momentum_hbm,
                  updates_hbm, held_ref, partial_ref, base_ref, log_ref, limit_ref, member_ref,
                  log_s, cohort_s, seeds_s, momentum_v, sums_v, small_sems, sems):
    local_clients, row_count, _ = held_ref.shape
    rows, cols = momentum_v.shape
    cohort_count = log_s.shape[0]
    total_clients = cohort_s.shape[0]
    small = []
    for k, (source, target) in enumerate((
        (seeds_hbm, seeds_s), (log_hbm, log_s), (cohort_hbm, cohort_s), (momentum_hbm, momentum_v),
    )):
        small.append(pltpu.make_async_copy(source, target, small_sems.at[k]))
        small[-1].start()
    for c in range(local_clients):
        pltpu.make_async_copy(updates_hbm.at[c], held_ref.at[c], sems.at[c]).start()
    for copy in small:
        copy.wait()

    lanes = lane_ids((1, LANES))
    own = lax.axis_index("client") * local_clients
    logs = jnp.full((1, LANES), log_s[0], jnp.float32)
    for g in range(1, cohort_count):
        logs = jnp.where(lanes == g, log_s[g], logs)
    log_ref[...] = logs
    largest = jnp.max(jnp.exp(logs), axis=1, keepdims=True)
    own_logs = jnp.zeros((1, LANES), jnp.float32)
    for c in range(local_clients):
        cohort = cohort_s[own + c]
        own_logs = jnp.where(lanes == c, log_s[cohort], own_logs)
        member_ref[c : c + 1, :] = jnp.where(lanes % HALF == cohort, 1.0, 0.0)
    limit_ref[...] = jnp.exp(own_logs)

    first_row = lax.axis_index("shard") * rows
    first_col = lax.axis_index("client") * cols
    row_ids = first_row + lax.broadcasted_iota(jnp.int32, (rows, cols), 0)
    col_ids = first_col + lax.broadcasted_iota(jnp.int32, (rows, cols), 1)
    spread = (row_ids * jnp.int32(width) + col_ids) * jnp.int32(1013904223)
    rate = 0.4 + 0.07 * jnp.full((1, 1), coef_s[0], jnp.int32).astype(jnp.float32)
    coef = jnp.ones((1, 1), jnp.float32)
    noise = jnp.zeros((rows, cols), jnp.float32)
    for j in range(seeds_s.shape[0]):
        if j:
            coef = coef * (rate * ((2.0 * j - 1.0) / (2.0 * j)))
        key = mix(seeds_s[j] ^ ((round_s[0] - j) * jnp.int32(1640531527)))
        hashed = mix(spread + key)
        uniform = (lax.shift_right_logical(hashed, jnp.int32(8)).astype(jnp.float32) + 0.5) * (
            1.0 / 16777216.0
        )
        noise = noise + coef * (3.4641016151377544 * (uniform - 0.5))
    base_ref[...] = 0.9 * momentum_v[...] + (0.05 * largest * noise) / total_clients

    step = 2 * GROUPS * LANES

    def add_client(c, carry):
        pltpu.make_async_copy(updates_hbm.at[c], held_ref.at[c], sems.at[c]).wait()
        acc = jnp.zeros((row_count, step), jnp.float32)
        for at in range(0, width, step):
            block = held_ref[c, :, at : at + step].astype(jnp.float32)
            acc = acc + block * block
        sums_v[c] = fold(acc)
        return carry

    lax.fori_loop(0, local_clients, add_client, 0)
    column = jnp.sum(jnp.sum(sums_v[...], axis=1), axis=1, keepdims=True)
    row = jnp.sum(jnp.where(diagonal(local_clients), column, 0.0), axis=0, keepdims=True)
    partial_ref[...] = jnp.broadcast_to(row[None], partial_ref.shape)


def weight_kernel(limit_ref, member_ref, squares_ref, held_ref, slab_ref):
    local_clients, row_count, width = held_ref.shape
    step = 2 * GROUPS * LANES
    norms = jnp.sqrt(jnp.sum(squares_ref[...], axis=0))
    limit = limit_ref[...]
    factor = limit / jnp.maximum(norms, limit)
    factors = [jnp.broadcast_to(factor[:, c : c + 1], (row_count, step)) for c in range(local_clients)]
    bit = (norms <= limit).astype(jnp.float32)
    bits = jnp.sum(jnp.where(diagonal(local_clients), bit, 0.0), axis=1, keepdims=True)
    counts = jnp.sum(member_ref[...] * bits, axis=0, keepdims=True)
    eight = (8, LANES)
    counts = jnp.where(lax.broadcasted_iota(jnp.int32, eight, 0) == 0, counts, 0.0)
    left = lane_ids(eight) < HALF

    def pairs(p, carry):
        at = pl.multiple_of(p * step, step)
        acc = jnp.zeros((row_count, step), jnp.float32)
        for c in range(local_clients):
            acc = acc + held_ref[c, :, pl.ds(at, step)].astype(jnp.float32) * factors[c]
        for k in range(4):
            def group(j, rows):
                first = ((k // 2) * GROUPS + j) * LANES
                return acc[rows, first : first + LANES]

            names = ODD if k % 2 else EVEN
            upper = [group(j, slice(0, 8)) for j in names]
            lower = [group(j, slice(8, 12)) for j in names]
            upper[3] = jnp.where(left, counts, upper[3]) if k % 2 else jnp.where(left, upper[3], counts)
            for j in range(4):
                slab_ref[4 * p + k, :, j * LANES : (j + 1) * LANES] = upper[j]
            for j in range(2):
                slab_ref[4 * p + k, :, (4 + j) * LANES : (5 + j) * LANES] = jnp.concatenate(
                    [lower[j], lower[j + 2]], axis=0
                )
        return carry

    lax.fori_loop(0, width // step, pairs, 0, unroll=2)


def own_columns(x, odd):
    as_odd = jnp.concatenate([x[:, 3 * LANES + HALF :], x[:, : 3 * LANES]], axis=1)
    return jnp.where(odd, as_odd, x[:, : 3 * LANES + HALF])


def finish_kernel(total_clients, cohort_count, log_ref, base_ref, slab_ref, momentum_ref, next_ref):
    odd = lax.axis_index("client") % 2 == 1
    total = jnp.sum(slab_ref[...], axis=0)
    upper = total[:, : 4 * LANES]
    lower = jnp.concatenate([total[:4, 4 * LANES :], total[4:, 4 * LANES :]], axis=1)
    momentum_ref[:8, :] = base_ref[:8, :] + own_columns(upper, odd) / total_clients
    momentum_ref[8:, :] = base_ref[8:, :] + own_columns(lower, odd) / total_clients
    middle = upper[:1, 3 * LANES :]
    counts = jnp.where(odd, middle[:, :cohort_count], middle[:, HALF : HALF + cohort_count])
    next_ref[...] = log_ref[:, :cohort_count] - 0.2 * (counts / (total_clients // cohort_count) - 0.5)


def per_device(updates, momentum, log_thresholds, cohort_of, seeds, round_index, coef_index):
    local_clients, _, width = updates.shape
    rows, cols = momentum.shape
    cohort_count = log_thresholds.shape[0]
    total_clients = cohort_of.shape[0]
    shards = lax.axis_size("shard")
    owners = lax.axis_size("client")
    vmem = pl.BlockSpec(memory_space=pltpu.VMEM)
    hbm = pl.BlockSpec(memory_space=pltpu.HBM)
    smem = pl.BlockSpec(memory_space=pltpu.SMEM)
    params = pltpu.CompilerParams(vmem_limit_bytes=24 * MIB)

    def square(*refs):
        square_kernel(width, *refs)

    held, partial, base, log_row, limit, member = pl.pallas_call(
        square,
        out_shape=(
            pltpu.VMEM(updates.shape, jnp.bfloat16),
            jax.ShapeDtypeStruct((shards, 1, LANES), jnp.float32),
            jax.ShapeDtypeStruct((rows, cols), jnp.float32),
            jax.ShapeDtypeStruct((1, LANES), jnp.float32),
            jax.ShapeDtypeStruct((1, LANES), jnp.float32),
            jax.ShapeDtypeStruct((local_clients, LANES), jnp.float32),
        ),
        in_specs=[smem] * 2 + [hbm] * 5,
        out_specs=(vmem,) * 6,
        scratch_shapes=[
            pltpu.SMEM((cohort_count,), jnp.float32),
            pltpu.SMEM((total_clients,), jnp.int32),
            pltpu.SMEM(seeds.shape, jnp.int32),
            pltpu.VMEM((rows, cols), jnp.float32),
            pltpu.VMEM((local_clients, rows, LANES), jnp.float32),
            pltpu.SemaphoreType.DMA((4,)),
            pltpu.SemaphoreType.DMA((local_clients,)),
        ],
        compiler_params=params,
        name="squares",
    )(round_index, coef_index, *(
        pltpu.with_memory_space_constraint(x, pltpu.HBM)
        for x in (log_thresholds, cohort_of, seeds, momentum, updates)
    ))

    squares = lax.all_to_all(partial, "shard", 0, 0, tiled=True)

    slabs = pl.pallas_call(
        weight_kernel,
        out_shape=jax.ShapeDtypeStruct((owners, 8, SLAB), jnp.float32),
        in_specs=[vmem] * 4,
        out_specs=vmem,
        compiler_params=params,
        name="weighted_sum",
    )(limit, member, squares, held)

    parts = lax.all_to_all(slabs, "client", 0, 0, tiled=True)

    def finish(*refs):
        finish_kernel(total_clients, cohort_count, *refs)

    momentum_next, log_next = pl.pallas_call(
        finish,
        out_shape=(
            jax.ShapeDtypeStruct((rows, cols), jnp.float32),
            jax.ShapeDtypeStruct((1, cohort_count), jnp.float32),
        ),
        in_specs=[vmem] * 3,
        out_specs=(vmem,) * 2,
        compiler_params=params,
        name="finish",
    )(log_row, base, parts)
    return (momentum_next, log_next.reshape(cohort_count))


def solution(mesh):
    placed = (P("client", "shard", None), P("shard", "client"), P(), P(), P(), P(), P())
    return jax.shard_map(
        per_device,
        mesh=mesh,
        in_specs=placed,
        out_specs=(P("shard", "client"), P()),
        check_vma=False,
    )
```

```python
import jax
import jax.numpy as jnp
from jax import lax
from jax.experimental import pallas as pl
from jax.experimental.pallas import tpu as pltpu
from jax.sharding import PartitionSpec as P

LANES = 128
HALF = LANES // 2
MIB = 1024 * 1024

PAIR = 7 * LANES
REACH = 4 * LANES
SLAB = 6 * LANES


def mix(x):
    x = x ^ lax.shift_right_logical(x, jnp.int32(16))
    x = x * jnp.int32(2146121005)
    x = x ^ lax.shift_right_logical(x, jnp.int32(15))
    x = x * jnp.int32(-2073450869)
    x = x ^ lax.shift_right_logical(x, jnp.int32(16))
    return x


def lane_ids(shape):
    return lax.broadcasted_iota(jnp.int32, shape, len(shape) - 1)


def row_ids(shape):
    return lax.broadcasted_iota(jnp.int32, shape, len(shape) - 2)


def diagonal(size):
    return row_ids((size, LANES)) == lane_ids((size, LANES))


def fold(x):
    parts = [x[:, at : at + LANES] for at in range(0, x.shape[1], LANES)]
    while len(parts) > 1:
        parts = [sum(parts[at : at + 2]) for at in range(0, len(parts), 2)]
    return parts[0]


def square_kernel(log_hbm, cohort_hbm, seeds_hbm, momentum_hbm, updates_hbm,
                  held_ref, partial_ref, momentum_ref, seeds_ref, log_ref, limit_ref, member_ref,
                  log_s, cohort_s, seeds_s, sums_v, small_sems, sems):
    local_clients, row_count, width = held_ref.shape
    cohort_count = log_s.shape[0]
    small = []
    for k, (source, target) in enumerate((
        (log_hbm, log_s), (cohort_hbm, cohort_s), (seeds_hbm, seeds_s), (momentum_hbm, momentum_ref),
    )):
        small.append(pltpu.make_async_copy(source, target, small_sems.at[k]))
        small[-1].start()
    for c in range(local_clients):
        pltpu.make_async_copy(updates_hbm.at[c], held_ref.at[c], sems.at[c]).start()
    for copy in small:
        copy.wait()

    lanes = lane_ids((1, LANES))
    own = lax.axis_index("client") * local_clients
    logs = jnp.full((1, LANES), log_s[0], jnp.float32)
    for g in range(1, cohort_count):
        logs = jnp.where(lanes == g, log_s[g], logs)
    log_ref[...] = logs
    seed_row = jnp.zeros((1, LANES), jnp.int32)
    for j in range(seeds_s.shape[0]):
        seed_row = jnp.where(lanes == j, seeds_s[j], seed_row)
    seeds_ref[...] = seed_row
    own_logs = jnp.zeros((1, LANES), jnp.float32)
    for c in range(local_clients):
        cohort = cohort_s[own + c]
        own_logs = jnp.where(lanes == c, log_s[cohort], own_logs)
        member_ref[c : c + 1, :] = jnp.where((lanes & (HALF - 1)) == cohort, 1.0, 0.0)
    limit_ref[...] = jnp.exp(own_logs)

    step = 2 * PAIR

    def add_client(c, carry):
        pltpu.make_async_copy(updates_hbm.at[c], held_ref.at[c], sems.at[c]).wait()
        acc = jnp.zeros((row_count, step), jnp.float32)
        for at in range(0, width, step):
            block = held_ref[c, :, at : at + step].astype(jnp.float32)
            acc = acc + block * block
        sums_v[c] = fold(acc)
        return carry

    lax.fori_loop(0, local_clients, add_client, 0)
    column = jnp.sum(jnp.sum(sums_v[...], axis=1), axis=1, keepdims=True)
    row = jnp.sum(jnp.where(diagonal(local_clients), column, 0.0), axis=0, keepdims=True)
    partial_ref[...] = jnp.broadcast_to(row[None], partial_ref.shape)


def weight_kernel(other, limit_ref, member_ref, squares_ref, held_ref, slab_ref):
    local_clients, row_count, width = held_ref.shape
    odd = (lax.axis_index("client") + other) % 2
    norms = jnp.sqrt(jnp.sum(squares_ref[...], axis=0))
    limit = limit_ref[...]
    factor = limit / jnp.maximum(norms, limit)
    factors = [jnp.broadcast_to(factor[:, c : c + 1], (row_count, REACH)) for c in range(local_clients)]
    bit = (norms <= limit).astype(jnp.float32)
    bits = jnp.sum(jnp.where(diagonal(local_clients), bit, 0.0), axis=1, keepdims=True)
    counts = jnp.sum(member_ref[...] * bits, axis=0, keepdims=True)
    eight = (8, LANES)
    counts = jnp.where(row_ids(eight) == 0, counts, 0.0)
    left = lane_ids(eight) < HALF
    spare_first = left & (odd == 1)
    spare_last = jnp.logical_not(left) & (odd == 0)

    def pair(p, carry):
        at = pl.multiple_of(p * PAIR + odd * (PAIR - REACH), LANES)
        acc = jnp.zeros((row_count, REACH), jnp.float32)
        for c in range(local_clients):
            acc = acc + held_ref[c, :, pl.ds(at, REACH)].astype(jnp.float32) * factors[c]
        upper = [acc[:8, j * LANES : (j + 1) * LANES] for j in range(4)]
        lower = [acc[8:, j * LANES : (j + 1) * LANES] for j in range(4)]
        upper[0] = jnp.where(spare_first, counts, upper[0])
        upper[3] = jnp.where(spare_last, counts, upper[3])
        for j in range(4):
            slab_ref[p, :, j * LANES : (j + 1) * LANES] = upper[j]
        for j in range(2):
            slab_ref[p, :, (4 + j) * LANES : (5 + j) * LANES] = jnp.concatenate(
                [lower[j], lower[j + 2]], axis=0
            )
        return carry

    lax.fori_loop(0, width // PAIR, pair, 0, unroll=4)


def base_kernel(width, total_clients, band, round_s, coef_s, seeds_ref, log_ref, momentum_ref, base_ref):
    rows, cols = momentum_ref.shape
    first_row = lax.axis_index("shard") * rows
    first_col = lax.axis_index("client") * cols
    block = (rows, cols)
    index = (first_row + row_ids(block)) * jnp.int32(width) + (first_col + lane_ids(block))
    spread = index * jnp.int32(1013904223)
    keys = mix(seeds_ref[...] ^ ((round_s[0] - lane_ids((1, LANES))) * jnp.int32(1640531527)))
    rate = 0.4 + 0.07 * jnp.full((1, 1), coef_s[0], jnp.int32).astype(jnp.float32)
    coef = jnp.ones((1, 1), jnp.float32)
    noise = jnp.zeros(block, jnp.float32)
    for j in range(band):
        if j:
            coef = coef * (rate * ((2.0 * j - 1.0) / (2.0 * j)))
        hashed = mix(spread + keys[:, j : j + 1])
        uniform = (lax.shift_right_logical(hashed, jnp.int32(8)).astype(jnp.float32) + 0.5) * (
            1.0 / 16777216.0
        )
        noise = noise + coef * (3.4641016151377544 * (uniform - 0.5))
    largest = jnp.max(jnp.exp(log_ref[...]), axis=1, keepdims=True)
    base_ref[...] = 0.9 * momentum_ref[...] + (0.05 * largest * noise) / total_clients


def finish_kernel(total_clients, cohort_count, log_ref, base_ref, slab_ref, momentum_ref, next_ref):
    cols = base_ref.shape[1]
    odd = lax.axis_index("client") % 2 == 1
    total = jnp.sum(slab_ref[...], axis=0)
    upper = total[:, :REACH]
    lower = jnp.concatenate([total[:4, REACH:], total[4:, REACH:]], axis=1)
    upper_own = jnp.where(odd, upper[:, HALF:], upper[:, :cols])
    lower_own = jnp.where(odd, lower[:, HALF:], lower[:, :cols])
    momentum_ref[:8, :] = base_ref[:8, :] + upper_own / total_clients
    momentum_ref[8:, :] = base_ref[8:, :] + lower_own / total_clients
    counts = jnp.where(odd, upper[:1, :cohort_count], upper[:1, cols : cols + cohort_count])
    next_ref[...] = log_ref[:, :cohort_count] - 0.2 * (counts / (total_clients // cohort_count) - 0.5)


def per_device(updates, momentum, log_thresholds, cohort_of, seeds, round_index, coef_index):
    local_clients, _, width = updates.shape
    rows, cols = momentum.shape
    cohort_count = log_thresholds.shape[0]
    total_clients = cohort_of.shape[0]
    shards = lax.axis_size("shard")
    owners = lax.axis_size("client")
    chips = owners // 2
    vmem = pl.BlockSpec(memory_space=pltpu.VMEM)
    hbm = pl.BlockSpec(memory_space=pltpu.HBM)
    smem = pl.BlockSpec(memory_space=pltpu.SMEM)
    params = pltpu.CompilerParams(vmem_limit_bytes=24 * MIB)
    row = jax.ShapeDtypeStruct((1, LANES), jnp.float32)

    held, partial, momentum_v, seed_row, log_row, limit, member = pl.pallas_call(
        square_kernel,
        out_shape=(
            pltpu.VMEM(updates.shape, jnp.bfloat16),
            jax.ShapeDtypeStruct((shards, 1, LANES), jnp.float32),
            pltpu.VMEM((rows, cols), jnp.float32),
            jax.ShapeDtypeStruct((1, LANES), jnp.int32),
            row,
            row,
            jax.ShapeDtypeStruct((local_clients, LANES), jnp.float32),
        ),
        in_specs=[hbm] * 5,
        out_specs=(vmem,) * 7,
        scratch_shapes=[
            pltpu.SMEM((cohort_count,), jnp.float32),
            pltpu.SMEM((total_clients,), jnp.int32),
            pltpu.SMEM(seeds.shape, jnp.int32),
            pltpu.VMEM((local_clients, rows, LANES), jnp.float32),
            pltpu.SemaphoreType.DMA((4,)),
            pltpu.SemaphoreType.DMA((local_clients,)),
        ],
        compiler_params=params,
        name="squares",
    )(*(
        pltpu.with_memory_space_constraint(x, pltpu.HBM)
        for x in (log_thresholds, cohort_of, seeds, momentum, updates)
    ))

    squares = lax.all_to_all(partial, "shard", 0, 0, tiled=True)

    def weighted(other):
        def weight(*refs):
            weight_kernel(other, *refs)

        return pl.pallas_call(
            weight,
            out_shape=jax.ShapeDtypeStruct((chips, 8, SLAB), jnp.float32),
            in_specs=[vmem] * 4,
            out_specs=vmem,
            compiler_params=params,
            cost_estimate=pl.CostEstimate(
                flops=2 * updates.size, bytes_accessed=updates.size, transcendentals=0
            ),
            name="weighted_theirs" if other else "weighted_own",
        )(limit, member, squares, held)

    theirs = weighted(1)
    theirs, round_index, coef_index = lax.optimization_barrier((theirs, round_index, coef_index))
    arrived = lax.ppermute(theirs, "client", [(i, i ^ 1) for i in range(owners)])
    own = weighted(0)

    def base_of(*refs):
        base_kernel(width, total_clients, seeds.shape[0], *refs)

    base = pl.pallas_call(
        base_of,
        out_shape=jax.ShapeDtypeStruct((rows, cols), jnp.float32),
        in_specs=[smem] * 2 + [vmem] * 3,
        out_specs=vmem,
        compiler_params=params,
        cost_estimate=pl.CostEstimate(
            flops=200 * momentum.size, bytes_accessed=8 * momentum.size, transcendentals=0
        ),
        name="base",
    )(round_index, coef_index, seed_row, log_row, momentum_v)

    parts = lax.all_to_all(
        own + arrived, "client", 0, 0, tiled=True,
        axis_index_groups=[[2 * i + core for i in range(chips)] for core in range(2)],
    )

    def finish(*refs):
        finish_kernel(total_clients, cohort_count, *refs)

    momentum_next, log_next = pl.pallas_call(
        finish,
        out_shape=(
            jax.ShapeDtypeStruct((rows, cols), jnp.float32),
            jax.ShapeDtypeStruct((1, cohort_count), jnp.float32),
        ),
        in_specs=[vmem] * 3,
        out_specs=(vmem,) * 2,
        compiler_params=params,
        name="finish",
    )(log_row, base, parts)
    return (momentum_next, log_next.reshape(cohort_count))


def solution(mesh):
    placed = (P("client", "shard", None), P("shard", "client"), P(), P(), P(), P(), P())
    return jax.shard_map(
        per_device,
        mesh=mesh,
        in_specs=placed,
        out_specs=(P("shard", "client"), P()),
        check_vma=False,
    )
```

```python
import jax
import jax.numpy as jnp
from jax import lax
from jax.experimental import pallas as pl
from jax.experimental.pallas import tpu as pltpu
from jax.sharding import Mesh, PartitionSpec as P

LANES = 128
HALF = LANES // 2
MIB = 1024 * 1024

PAIR = 7 * LANES
REACH = 4 * LANES
SLAB = 6 * LANES


def mix(x):
    x = x ^ lax.shift_right_logical(x, jnp.int32(16))
    x = x * jnp.int32(2146121005)
    x = x ^ lax.shift_right_logical(x, jnp.int32(15))
    x = x * jnp.int32(-2073450869)
    x = x ^ lax.shift_right_logical(x, jnp.int32(16))
    return x


def lane_ids(shape):
    return lax.broadcasted_iota(jnp.int32, shape, len(shape) - 1)


def row_ids(shape):
    return lax.broadcasted_iota(jnp.int32, shape, len(shape) - 2)


def diagonal(size):
    return row_ids((size, LANES)) == lane_ids((size, LANES))


def fold(x):
    parts = [x[:, at : at + LANES] for at in range(0, x.shape[1], LANES)]
    while len(parts) > 1:
        parts = [sum(parts[at : at + 2]) for at in range(0, len(parts), 2)]
    return parts[0]


def square_kernel(log_hbm, cohort_hbm, seeds_hbm, momentum_hbm, updates_hbm,
                  held_ref, partial_ref, momentum_ref, seeds_ref, log_ref, limit_ref, member_ref,
                  log_s, cohort_s, seeds_s, sums_v, small_sems, sems):
    local_clients, row_count, width = held_ref.shape
    cohort_count = log_s.shape[0]
    small = []
    for k, (source, target) in enumerate((
        (log_hbm, log_s), (cohort_hbm, cohort_s), (seeds_hbm, seeds_s), (momentum_hbm, momentum_ref),
    )):
        small.append(pltpu.make_async_copy(source, target, small_sems.at[k]))
        small[-1].start()
    for c in range(local_clients):
        pltpu.make_async_copy(updates_hbm.at[c], held_ref.at[c], sems.at[c]).start()
    for copy in small:
        copy.wait()

    lanes = lane_ids((1, LANES))
    own = (2 * lax.axis_index("chip") + lax.axis_index("core")) * local_clients
    logs = jnp.full((1, LANES), log_s[0], jnp.float32)
    for g in range(1, cohort_count):
        logs = jnp.where(lanes == g, log_s[g], logs)
    log_ref[...] = logs
    seed_row = jnp.zeros((1, LANES), jnp.int32)
    for j in range(seeds_s.shape[0]):
        seed_row = jnp.where(lanes == j, seeds_s[j], seed_row)
    seeds_ref[...] = seed_row
    own_logs = jnp.zeros((1, LANES), jnp.float32)
    for c in range(local_clients):
        cohort = cohort_s[own + c]
        own_logs = jnp.where(lanes == c, log_s[cohort], own_logs)
        member_ref[c : c + 1, :] = jnp.where((lanes & (HALF - 1)) == cohort, 1.0, 0.0)
    limit_ref[...] = jnp.exp(own_logs)

    step = 2 * PAIR

    def add_client(c, carry):
        pltpu.make_async_copy(updates_hbm.at[c], held_ref.at[c], sems.at[c]).wait()
        acc = jnp.zeros((row_count, step), jnp.float32)
        for at in range(0, width, step):
            block = held_ref[c, :, at : at + step].astype(jnp.float32)
            acc = acc + block * block
        sums_v[c] = fold(acc)
        return carry

    lax.fori_loop(0, local_clients, add_client, 0)
    column = jnp.sum(jnp.sum(sums_v[...], axis=1), axis=1, keepdims=True)
    row = jnp.sum(jnp.where(diagonal(local_clients), column, 0.0), axis=0, keepdims=True)
    partial_ref[...] = jnp.broadcast_to(row[None], partial_ref.shape)


def weight_kernel(other, limit_ref, member_ref, squares_ref, held_ref, slab_ref):
    local_clients, row_count, width = held_ref.shape
    odd = (lax.axis_index("core") + other) % 2
    norms = jnp.sqrt(jnp.sum(squares_ref[...], axis=0))
    limit = limit_ref[...]
    factor = limit / jnp.maximum(norms, limit)
    factors = [jnp.broadcast_to(factor[:, c : c + 1], (row_count, REACH)) for c in range(local_clients)]
    bit = (norms <= limit).astype(jnp.float32)
    bits = jnp.sum(jnp.where(diagonal(local_clients), bit, 0.0), axis=1, keepdims=True)
    counts = jnp.sum(member_ref[...] * bits, axis=0, keepdims=True)
    eight = (8, LANES)
    counts = jnp.where(row_ids(eight) == 0, counts, 0.0)
    left = lane_ids(eight) < HALF
    spare_first = left & (odd == 1)
    spare_last = jnp.logical_not(left) & (odd == 0)

    def pair(p, carry):
        at = pl.multiple_of(p * PAIR + odd * (PAIR - REACH), LANES)
        acc = jnp.zeros((row_count, REACH), jnp.float32)
        for c in range(local_clients):
            acc = acc + held_ref[c, :, pl.ds(at, REACH)].astype(jnp.float32) * factors[c]
        upper = [acc[:8, j * LANES : (j + 1) * LANES] for j in range(4)]
        lower = [acc[8:, j * LANES : (j + 1) * LANES] for j in range(4)]
        upper[0] = jnp.where(spare_first, counts, upper[0])
        upper[3] = jnp.where(spare_last, counts, upper[3])
        for j in range(4):
            slab_ref[p, :, j * LANES : (j + 1) * LANES] = upper[j]
        for j in range(2):
            slab_ref[p, :, (4 + j) * LANES : (5 + j) * LANES] = jnp.concatenate(
                [lower[j], lower[j + 2]], axis=0
            )
        return carry

    lax.fori_loop(0, width // PAIR, pair, 0, unroll=4)


def base_kernel(width, total_clients, band, round_s, coef_s, seeds_ref, log_ref, momentum_ref, base_ref):
    rows, cols = momentum_ref.shape
    first_row = lax.axis_index("shard") * rows
    first_col = (2 * lax.axis_index("chip") + lax.axis_index("core")) * cols
    block = (rows, cols)
    index = (first_row + row_ids(block)) * jnp.int32(width) + (first_col + lane_ids(block))
    spread = index * jnp.int32(1013904223)
    keys = mix(seeds_ref[...] ^ ((round_s[0] - lane_ids((1, LANES))) * jnp.int32(1640531527)))
    rate = 0.4 + 0.07 * jnp.full((1, 1), coef_s[0], jnp.int32).astype(jnp.float32)
    coef = jnp.ones((1, 1), jnp.float32)
    noise = jnp.zeros(block, jnp.float32)
    for j in range(band):
        if j:
            coef = coef * (rate * ((2.0 * j - 1.0) / (2.0 * j)))
        hashed = mix(spread + keys[:, j : j + 1])
        uniform = (lax.shift_right_logical(hashed, jnp.int32(8)).astype(jnp.float32) + 0.5) * (
            1.0 / 16777216.0
        )
        noise = noise + coef * (3.4641016151377544 * (uniform - 0.5))
    largest = jnp.max(jnp.exp(log_ref[...]), axis=1, keepdims=True)
    base_ref[...] = 0.9 * momentum_ref[...] + (0.05 * largest * noise) / total_clients


def add_kernel(one_ref, other_ref, sum_ref):
    sum_ref[...] = one_ref[...] + other_ref[...]


def finish_kernel(total_clients, cohort_count, log_ref, base_ref, slab_ref, momentum_ref, next_ref):
    cols = base_ref.shape[1]
    odd = lax.axis_index("core") == 1
    total = jnp.sum(slab_ref[...], axis=0)
    upper = total[:, :REACH]
    lower = jnp.concatenate([total[:4, REACH:], total[4:, REACH:]], axis=1)
    upper_own = jnp.where(odd, upper[:, HALF:], upper[:, :cols])
    lower_own = jnp.where(odd, lower[:, HALF:], lower[:, :cols])
    momentum_ref[:8, :] = base_ref[:8, :] + upper_own / total_clients
    momentum_ref[8:, :] = base_ref[8:, :] + lower_own / total_clients
    counts = jnp.where(odd, upper[:1, :cohort_count], upper[:1, cols : cols + cohort_count])
    next_ref[...] = log_ref[:, :cohort_count] - 0.2 * (counts / (total_clients // cohort_count) - 0.5)


def per_device(updates, momentum, log_thresholds, cohort_of, seeds, round_index, coef_index):
    local_clients, _, width = updates.shape
    rows, cols = momentum.shape
    cohort_count = log_thresholds.shape[0]
    total_clients = cohort_of.shape[0]
    shards = lax.axis_size("shard")
    chips = lax.axis_size("chip")
    vmem = pl.BlockSpec(memory_space=pltpu.VMEM)
    hbm = pl.BlockSpec(memory_space=pltpu.HBM)
    smem = pl.BlockSpec(memory_space=pltpu.SMEM)
    params = pltpu.CompilerParams(vmem_limit_bytes=24 * MIB)
    row = jax.ShapeDtypeStruct((1, LANES), jnp.float32)

    held, partial, momentum_v, seed_row, log_row, limit, member = pl.pallas_call(
        square_kernel,
        out_shape=(
            pltpu.VMEM(updates.shape, jnp.bfloat16),
            jax.ShapeDtypeStruct((shards, 1, LANES), jnp.float32),
            pltpu.VMEM((rows, cols), jnp.float32),
            jax.ShapeDtypeStruct((1, LANES), jnp.int32),
            row,
            row,
            jax.ShapeDtypeStruct((local_clients, LANES), jnp.float32),
        ),
        in_specs=[hbm] * 5,
        out_specs=(vmem,) * 7,
        scratch_shapes=[
            pltpu.SMEM((cohort_count,), jnp.float32),
            pltpu.SMEM((total_clients,), jnp.int32),
            pltpu.SMEM(seeds.shape, jnp.int32),
            pltpu.VMEM((local_clients, rows, LANES), jnp.float32),
            pltpu.SemaphoreType.DMA((4,)),
            pltpu.SemaphoreType.DMA((local_clients,)),
        ],
        compiler_params=params,
        name="squares",
    )(*(
        pltpu.with_memory_space_constraint(x, pltpu.HBM)
        for x in (log_thresholds, cohort_of, seeds, momentum, updates)
    ))

    partial, round_index, coef_index = lax.optimization_barrier((partial, round_index, coef_index))
    squares = lax.all_to_all(
        partial, "shard", 0, 0, tiled=True, axis_index_groups=[list(range(shards))]
    )

    def weighted(other):
        def weight(*refs):
            weight_kernel(other, *refs)

        return pl.pallas_call(
            weight,
            out_shape=jax.ShapeDtypeStruct((chips, 8, SLAB), jnp.float32),
            in_specs=[vmem] * 4,
            out_specs=vmem,
            compiler_params=params,
            cost_estimate=pl.CostEstimate(
                flops=2 * updates.size, bytes_accessed=updates.size, transcendentals=0
            ),
            name="weighted_theirs" if other else "weighted_own",
        )(limit, member, squares, held)

    theirs = weighted(1)
    arrived = lax.ppermute(theirs, "core", [(0, 1), (1, 0)])
    own = weighted(0)

    def base_of(*refs):
        base_kernel(width, total_clients, seeds.shape[0], *refs)

    base = pl.pallas_call(
        base_of,
        out_shape=jax.ShapeDtypeStruct((rows, cols), jnp.float32),
        in_specs=[smem] * 2 + [vmem] * 3,
        out_specs=vmem,
        compiler_params=params,
        cost_estimate=pl.CostEstimate(
            flops=200 * momentum.size, bytes_accessed=8 * momentum.size, transcendentals=0
        ),
        name="base",
    )(round_index, coef_index, seed_row, log_row, momentum_v)

    both = pl.pallas_call(
        add_kernel,
        out_shape=jax.ShapeDtypeStruct(own.shape, jnp.float32),
        in_specs=[vmem] * 2,
        out_specs=vmem,
        compiler_params=params,
        name="add_cores",
    )(own, arrived)
    parts = lax.all_to_all(both, "chip", 0, 0, tiled=True)

    def finish(*refs):
        finish_kernel(total_clients, cohort_count, *refs)

    momentum_next, log_next = pl.pallas_call(
        finish,
        out_shape=(
            jax.ShapeDtypeStruct((rows, cols), jnp.float32),
            jax.ShapeDtypeStruct((1, cohort_count), jnp.float32),
        ),
        in_specs=[vmem] * 3,
        out_specs=(vmem,) * 2,
        compiler_params=params,
        name="finish",
    )(log_row, base, parts)
    return (momentum_next, log_next.reshape(cohort_count))


def solution(mesh):
    clients, shards = mesh.devices.shape
    split = Mesh(mesh.devices.reshape(clients // 2, 2, shards), ("chip", "core", "shard"))
    client = ("chip", "core")
    return jax.shard_map(
        per_device,
        mesh=split,
        in_specs=(P(client, "shard", None), P("shard", client), P(), P(), P(), P(), P()),
        out_specs=(P("shard", client), P()),
        check_vma=False,
    )
```

```python
import jax
import jax.numpy as jnp
from jax import lax
from jax.experimental import pallas as pl
from jax.experimental.pallas import tpu as pltpu
from jax.sharding import Mesh, PartitionSpec as P

LANES = 128
HALF = LANES // 2
MIB = 1024 * 1024

PAIR = 7 * LANES
REACH = 4 * LANES
SLAB = 6 * LANES


def mix(x):
    x = x ^ lax.shift_right_logical(x, jnp.int32(16))
    x = x * jnp.int32(2146121005)
    x = x ^ lax.shift_right_logical(x, jnp.int32(15))
    x = x * jnp.int32(-2073450869)
    x = x ^ lax.shift_right_logical(x, jnp.int32(16))
    return x


def lane_ids(shape):
    return lax.broadcasted_iota(jnp.int32, shape, len(shape) - 1)


def row_ids(shape):
    return lax.broadcasted_iota(jnp.int32, shape, len(shape) - 2)


def diagonal(size):
    return row_ids((size, LANES)) == lane_ids((size, LANES))


def fold(x):
    parts = [x[:, at : at + LANES] for at in range(0, x.shape[1], LANES)]
    while len(parts) > 1:
        parts = [sum(parts[at : at + 2]) for at in range(0, len(parts), 2)]
    return parts[0]


def square_kernel(log_hbm, cohort_hbm, seeds_hbm, momentum_hbm, updates_hbm,
                  held_ref, partial_ref, momentum_ref, seeds_ref, log_ref, limit_ref, member_ref,
                  log_s, cohort_s, seeds_s, sums_v, small_sems, sems):
    local_clients, row_count, width = held_ref.shape
    cohort_count = log_s.shape[0]
    small = []
    for k, (source, target) in enumerate((
        (log_hbm, log_s), (cohort_hbm, cohort_s), (seeds_hbm, seeds_s), (momentum_hbm, momentum_ref),
    )):
        small.append(pltpu.make_async_copy(source, target, small_sems.at[k]))
        small[-1].start()
    for c in range(local_clients):
        pltpu.make_async_copy(updates_hbm.at[c], held_ref.at[c], sems.at[c]).start()
    for copy in small:
        copy.wait()

    lanes = lane_ids((1, LANES))
    own = (2 * lax.axis_index("chip") + lax.axis_index("core")) * local_clients
    logs = jnp.full((1, LANES), log_s[0], jnp.float32)
    for g in range(1, cohort_count):
        logs = jnp.where(lanes == g, log_s[g], logs)
    log_ref[...] = logs
    seed_row = jnp.zeros((1, LANES), jnp.int32)
    for j in range(seeds_s.shape[0]):
        seed_row = jnp.where(lanes == j, seeds_s[j], seed_row)
    seeds_ref[...] = seed_row
    own_logs = jnp.zeros((1, LANES), jnp.float32)
    for c in range(local_clients):
        cohort = cohort_s[own + c]
        own_logs = jnp.where(lanes == c, log_s[cohort], own_logs)
        member_ref[c : c + 1, :] = jnp.where((lanes & (HALF - 1)) == cohort, 1.0, 0.0)
    limit_ref[...] = jnp.exp(own_logs)

    step = 2 * PAIR

    def add_client(c, carry):
        pltpu.make_async_copy(updates_hbm.at[c], held_ref.at[c], sems.at[c]).wait()
        acc = jnp.zeros((row_count, step), jnp.float32)
        for at in range(0, width, step):
            block = held_ref[c, :, at : at + step].astype(jnp.float32)
            acc = acc + block * block
        sums_v[c] = fold(acc)
        return carry

    lax.fori_loop(0, local_clients, add_client, 0)
    column = jnp.sum(jnp.sum(sums_v[...], axis=1), axis=1, keepdims=True)
    row = jnp.sum(jnp.where(diagonal(local_clients), column, 0.0), axis=0, keepdims=True)
    partial_ref[...] = jnp.broadcast_to(row[None], partial_ref.shape)


def weight_kernel(other, limit_ref, member_ref, squares_ref, held_ref, slab_ref):
    local_clients, row_count, width = held_ref.shape
    odd = (lax.axis_index("core") + other) % 2
    norms = jnp.sqrt(jnp.sum(squares_ref[...], axis=0))
    limit = limit_ref[...]
    factor = limit / jnp.maximum(norms, limit)
    factors = [jnp.broadcast_to(factor[:, c : c + 1], (row_count, REACH)) for c in range(local_clients)]
    bit = (norms <= limit).astype(jnp.float32)
    bits = jnp.sum(jnp.where(diagonal(local_clients), bit, 0.0), axis=1, keepdims=True)
    counts = jnp.sum(member_ref[...] * bits, axis=0, keepdims=True)
    eight = (8, LANES)
    counts = jnp.where(row_ids(eight) == 0, counts, 0.0)
    left = lane_ids(eight) < HALF
    spare_first = left & (odd == 1)
    spare_last = jnp.logical_not(left) & (odd == 0)

    def pair(p, carry):
        at = pl.multiple_of(p * PAIR + odd * (PAIR - REACH), LANES)
        acc = jnp.zeros((row_count, REACH), jnp.float32)
        for c in range(local_clients):
            acc = acc + held_ref[c, :, pl.ds(at, REACH)].astype(jnp.float32) * factors[c]
        upper = [acc[:8, j * LANES : (j + 1) * LANES] for j in range(4)]
        lower = [acc[8:, j * LANES : (j + 1) * LANES] for j in range(4)]
        upper[0] = jnp.where(spare_first, counts, upper[0])
        upper[3] = jnp.where(spare_last, counts, upper[3])
        for j in range(4):
            slab_ref[p, :, j * LANES : (j + 1) * LANES] = upper[j]
        for j in range(2):
            slab_ref[p, :, (4 + j) * LANES : (5 + j) * LANES] = jnp.concatenate(
                [lower[j], lower[j + 2]], axis=0
            )
        return carry

    lax.fori_loop(0, width // PAIR, pair, 0, unroll=4)


def base_kernel(width, total_clients, band, round_s, coef_s, seeds_ref, log_ref, momentum_ref, base_ref):
    rows, cols = momentum_ref.shape
    first_row = lax.axis_index("shard") * rows
    first_col = (2 * lax.axis_index("chip") + lax.axis_index("core")) * cols
    block = (rows, cols)
    index = (first_row + row_ids(block)) * jnp.int32(width) + (first_col + lane_ids(block))
    spread = index * jnp.int32(1013904223)
    keys = mix(seeds_ref[...] ^ ((round_s[0] - lane_ids((1, LANES))) * jnp.int32(1640531527)))
    rate = 0.4 + 0.07 * jnp.full((1, 1), coef_s[0], jnp.int32).astype(jnp.float32)
    coef = jnp.ones((1, 1), jnp.float32)
    noise = jnp.zeros(block, jnp.float32)
    for j in range(band):
        if j:
            coef = coef * (rate * ((2.0 * j - 1.0) / (2.0 * j)))
        hashed = mix(spread + keys[:, j : j + 1])
        uniform = (lax.shift_right_logical(hashed, jnp.int32(8)).astype(jnp.float32) + 0.5) * (
            1.0 / 16777216.0
        )
        noise = noise + coef * (3.4641016151377544 * (uniform - 0.5))
    largest = jnp.max(jnp.exp(log_ref[...]), axis=1, keepdims=True)
    base_ref[...] = 0.9 * momentum_ref[...] + (0.05 * largest * noise) / total_clients


def add_kernel(one_ref, other_ref, sum_ref):
    sum_ref[...] = one_ref[...] + other_ref[...]


def finish_kernel(total_clients, cohort_count, log_ref, base_ref, slab_ref, momentum_ref, next_ref):
    cols = base_ref.shape[1]
    odd = lax.axis_index("core") == 1
    total = jnp.sum(slab_ref[...], axis=0)
    upper = total[:, :REACH]
    lower = jnp.concatenate([total[:4, REACH:], total[4:, REACH:]], axis=1)
    upper_own = jnp.where(odd, upper[:, HALF:], upper[:, :cols])
    lower_own = jnp.where(odd, lower[:, HALF:], lower[:, :cols])
    momentum_ref[:8, :] = base_ref[:8, :] + upper_own / total_clients
    momentum_ref[8:, :] = base_ref[8:, :] + lower_own / total_clients
    counts = jnp.where(odd, upper[:1, :cohort_count], upper[:1, cols : cols + cohort_count])
    next_ref[...] = log_ref[:, :cohort_count] - 0.2 * (counts / (total_clients // cohort_count) - 0.5)


def per_device(updates, momentum, log_thresholds, cohort_of, seeds, round_index, coef_index):
    local_clients, _, width = updates.shape
    rows, cols = momentum.shape
    cohort_count = log_thresholds.shape[0]
    total_clients = cohort_of.shape[0]
    shards = lax.axis_size("shard")
    chips = lax.axis_size("chip")
    vmem = pl.BlockSpec(memory_space=pltpu.VMEM)
    hbm = pl.BlockSpec(memory_space=pltpu.HBM)
    smem = pl.BlockSpec(memory_space=pltpu.SMEM)
    params = pltpu.CompilerParams(vmem_limit_bytes=24 * MIB)
    row = jax.ShapeDtypeStruct((1, LANES), jnp.float32)

    held, partial, momentum_v, seed_row, log_row, limit, member = pl.pallas_call(
        square_kernel,
        out_shape=(
            pltpu.VMEM(updates.shape, jnp.bfloat16),
            jax.ShapeDtypeStruct((shards, 1, LANES), jnp.float32),
            pltpu.VMEM((rows, cols), jnp.float32),
            jax.ShapeDtypeStruct((1, LANES), jnp.int32),
            row,
            row,
            jax.ShapeDtypeStruct((local_clients, LANES), jnp.float32),
        ),
        in_specs=[hbm] * 5,
        out_specs=(vmem,) * 7,
        scratch_shapes=[
            pltpu.SMEM((cohort_count,), jnp.float32),
            pltpu.SMEM((total_clients,), jnp.int32),
            pltpu.SMEM(seeds.shape, jnp.int32),
            pltpu.VMEM((local_clients, rows, LANES), jnp.float32),
            pltpu.SemaphoreType.DMA((4,)),
            pltpu.SemaphoreType.DMA((local_clients,)),
        ],
        compiler_params=params,
        name="squares",
    )(*(
        pltpu.with_memory_space_constraint(x, pltpu.HBM)
        for x in (log_thresholds, cohort_of, seeds, momentum, updates)
    ))

    partial, round_index, coef_index = lax.optimization_barrier((partial, round_index, coef_index))
    squares = lax.all_to_all(
        partial, "shard", 0, 0, tiled=True, axis_index_groups=[list(range(shards))]
    )

    def base_of(*refs):
        base_kernel(width, total_clients, seeds.shape[0], *refs)

    base = pl.pallas_call(
        base_of,
        out_shape=jax.ShapeDtypeStruct((rows, cols), jnp.float32),
        in_specs=[smem] * 2 + [vmem] * 3,
        out_specs=vmem,
        compiler_params=params,
        cost_estimate=pl.CostEstimate(
            flops=200 * momentum.size, bytes_accessed=8 * momentum.size, transcendentals=0
        ),
        name="base",
    )(round_index, coef_index, seed_row, log_row, momentum_v)

    def weighted(other):
        def weight(*refs):
            weight_kernel(other, *refs)

        return pl.pallas_call(
            weight,
            out_shape=jax.ShapeDtypeStruct((chips, 8, SLAB), jnp.float32),
            in_specs=[vmem] * 4,
            out_specs=vmem,
            compiler_params=params,
            cost_estimate=pl.CostEstimate(
                flops=2 * updates.size, bytes_accessed=updates.size, transcendentals=0
            ),
            name="weighted_theirs" if other else "weighted_own",
        )(limit, member, squares, held)

    theirs = weighted(1)
    arrived = lax.ppermute(theirs, "core", [(0, 1), (1, 0)])
    own = weighted(0)

    both = pl.pallas_call(
        add_kernel,
        out_shape=jax.ShapeDtypeStruct(own.shape, jnp.float32),
        in_specs=[vmem] * 2,
        out_specs=vmem,
        compiler_params=params,
        name="add_cores",
    )(own, arrived)
    both, base = lax.optimization_barrier((both, base))
    parts = lax.all_to_all(both, "chip", 0, 0, tiled=True)

    def finish(*refs):
        finish_kernel(total_clients, cohort_count, *refs)

    momentum_next, log_next = pl.pallas_call(
        finish,
        out_shape=(
            jax.ShapeDtypeStruct((rows, cols), jnp.float32),
            jax.ShapeDtypeStruct((1, cohort_count), jnp.float32),
        ),
        in_specs=[vmem] * 3,
        out_specs=(vmem,) * 2,
        compiler_params=params,
        name="finish",
    )(log_row, base, parts)
    return (momentum_next, log_next.reshape(cohort_count))


def solution(mesh):
    clients, shards = mesh.devices.shape
    split = Mesh(mesh.devices.reshape(clients // 2, 2, shards), ("chip", "core", "shard"))
    client = ("chip", "core")
    return jax.shard_map(
        per_device,
        mesh=split,
        in_specs=(P(client, "shard", None), P("shard", client), P(), P(), P(), P(), P()),
        out_specs=(P("shard", client), P()),
        check_vma=False,
    )
```

```python
import jax
import jax.numpy as jnp
from jax import lax
from jax.experimental import pallas as pl
from jax.experimental.pallas import tpu as pltpu
from jax.sharding import Mesh, PartitionSpec as P

LANES = 128
HALF = LANES // 2
MIB = 1024 * 1024

PAIR = 7 * LANES
REACH = 4 * LANES
SLAB = 6 * LANES


def mix(x):
    x = x ^ lax.shift_right_logical(x, jnp.int32(16))
    x = x * jnp.int32(2146121005)
    x = x ^ lax.shift_right_logical(x, jnp.int32(15))
    x = x * jnp.int32(-2073450869)
    x = x ^ lax.shift_right_logical(x, jnp.int32(16))
    return x


def lane_ids(shape):
    return lax.broadcasted_iota(jnp.int32, shape, len(shape) - 1)


def row_ids(shape):
    return lax.broadcasted_iota(jnp.int32, shape, len(shape) - 2)


def diagonal(size):
    return row_ids((size, LANES)) == lane_ids((size, LANES))


def fold(x):
    parts = [x[:, at : at + LANES] for at in range(0, x.shape[1], LANES)]
    while len(parts) > 1:
        parts = [sum(parts[at : at + 2]) for at in range(0, len(parts), 2)]
    return parts[0]


def square_kernel(log_hbm, cohort_hbm, seeds_hbm, momentum_hbm, updates_hbm,
                  held_ref, partial_ref, momentum_ref, seeds_ref, log_ref, limit_ref, member_ref,
                  log_s, cohort_s, seeds_s, sums_v, small_sems, sems):
    local_clients, row_count, width = held_ref.shape
    cohort_count = log_s.shape[0]
    def arrival(c):
        return pltpu.make_async_copy(updates_hbm.at[c], held_ref.at[c], sems.at[c])

    early = 2
    for c in range(early):
        arrival(c).start()
    small = []
    for k, (source, target) in enumerate((
        (log_hbm, log_s), (cohort_hbm, cohort_s), (seeds_hbm, seeds_s), (momentum_hbm, momentum_ref),
    )):
        small.append(pltpu.make_async_copy(source, target, small_sems.at[k]))
        small[-1].start()
    for c in range(early, local_clients):
        arrival(c).start()

    step = 2 * PAIR

    def add_client(c, carry):
        arrival(c).wait()
        acc = jnp.zeros((row_count, step), jnp.float32)
        for at in range(0, width, step):
            block = held_ref[c, :, at : at + step].astype(jnp.float32)
            acc = acc + block * block
        sums_v[c] = fold(acc)
        return carry

    lax.fori_loop(0, early, add_client, 0)
    for copy in small:
        copy.wait()

    lanes = lane_ids((1, LANES))
    own = (2 * lax.axis_index("chip") + lax.axis_index("core")) * local_clients
    logs = jnp.full((1, LANES), log_s[0], jnp.float32)
    for g in range(1, cohort_count):
        logs = jnp.where(lanes == g, log_s[g], logs)
    log_ref[...] = logs
    seed_row = jnp.zeros((1, LANES), jnp.int32)
    for j in range(seeds_s.shape[0]):
        seed_row = jnp.where(lanes == j, seeds_s[j], seed_row)
    seeds_ref[...] = seed_row
    own_logs = jnp.zeros((1, LANES), jnp.float32)
    for c in range(local_clients):
        cohort = cohort_s[own + c]
        own_logs = jnp.where(lanes == c, log_s[cohort], own_logs)
        member_ref[c : c + 1, :] = jnp.where((lanes & (HALF - 1)) == cohort, 1.0, 0.0)
    limit_ref[...] = jnp.exp(own_logs)

    lax.fori_loop(early, local_clients, add_client, 0)
    column = jnp.sum(jnp.sum(sums_v[...], axis=1), axis=1, keepdims=True)
    row = jnp.sum(jnp.where(diagonal(local_clients), column, 0.0), axis=0, keepdims=True)
    partial_ref[...] = jnp.broadcast_to(row[None], partial_ref.shape)


def weight_kernel(other, limit_ref, member_ref, squares_ref, held_ref, slab_ref):
    local_clients, row_count, width = held_ref.shape
    odd = (lax.axis_index("core") + other) % 2
    norms = jnp.sqrt(jnp.sum(squares_ref[...], axis=0))
    limit = limit_ref[...]
    factor = limit / jnp.maximum(norms, limit)
    factors = [jnp.broadcast_to(factor[:, c : c + 1], (row_count, REACH)) for c in range(local_clients)]
    bit = (norms <= limit).astype(jnp.float32)
    bits = jnp.sum(jnp.where(diagonal(local_clients), bit, 0.0), axis=1, keepdims=True)
    counts = jnp.sum(member_ref[...] * bits, axis=0, keepdims=True)
    eight = (8, LANES)
    counts = jnp.where(row_ids(eight) == 0, counts, 0.0)
    left = lane_ids(eight) < HALF
    spare_first = left & (odd == 1)
    spare_last = jnp.logical_not(left) & (odd == 0)

    def pair(p, carry):
        at = pl.multiple_of(p * PAIR + odd * (PAIR - REACH), LANES)
        acc = jnp.zeros((row_count, REACH), jnp.float32)
        for c in range(local_clients):
            acc = acc + held_ref[c, :, pl.ds(at, REACH)].astype(jnp.float32) * factors[c]
        upper = [acc[:8, j * LANES : (j + 1) * LANES] for j in range(4)]
        lower = [acc[8:, j * LANES : (j + 1) * LANES] for j in range(4)]
        upper[0] = jnp.where(spare_first, counts, upper[0])
        upper[3] = jnp.where(spare_last, counts, upper[3])
        for j in range(4):
            slab_ref[p, :, j * LANES : (j + 1) * LANES] = upper[j]
        for j in range(2):
            slab_ref[p, :, (4 + j) * LANES : (5 + j) * LANES] = jnp.concatenate(
                [lower[j], lower[j + 2]], axis=0
            )
        return carry

    lax.fori_loop(0, width // PAIR, pair, 0, unroll=4)


def base_kernel(width, total_clients, band, round_s, coef_s, seeds_ref, log_ref, momentum_ref, base_ref):
    rows, cols = momentum_ref.shape
    first_row = lax.axis_index("shard") * rows
    first_col = (2 * lax.axis_index("chip") + lax.axis_index("core")) * cols
    block = (rows, cols)
    index = (first_row + row_ids(block)) * jnp.int32(width) + (first_col + lane_ids(block))
    spread = index * jnp.int32(1013904223)
    keys = mix(seeds_ref[...] ^ ((round_s[0] - lane_ids((1, LANES))) * jnp.int32(1640531527)))
    rate = 0.4 + 0.07 * jnp.full((1, 1), coef_s[0], jnp.int32).astype(jnp.float32)
    coef = jnp.ones((1, 1), jnp.float32)
    noise = jnp.zeros(block, jnp.float32)
    for j in range(band):
        if j:
            coef = coef * (rate * ((2.0 * j - 1.0) / (2.0 * j)))
        hashed = mix(spread + keys[:, j : j + 1])
        uniform = (lax.shift_right_logical(hashed, jnp.int32(8)).astype(jnp.float32) + 0.5) * (
            1.0 / 16777216.0
        )
        noise = noise + coef * (3.4641016151377544 * (uniform - 0.5))
    largest = jnp.max(jnp.exp(log_ref[...]), axis=1, keepdims=True)
    base_ref[...] = 0.9 * momentum_ref[...] + (0.05 * largest * noise) / total_clients


def add_kernel(one_ref, other_ref, sum_ref):
    sum_ref[...] = one_ref[...] + other_ref[...]


def finish_kernel(total_clients, cohort_count, log_ref, base_ref, slab_ref, momentum_ref, next_ref):
    cols = base_ref.shape[1]
    odd = lax.axis_index("core") == 1
    total = jnp.sum(slab_ref[...], axis=0)
    upper = total[:, :REACH]
    lower = jnp.concatenate([total[:4, REACH:], total[4:, REACH:]], axis=1)
    upper_own = jnp.where(odd, upper[:, HALF:], upper[:, :cols])
    lower_own = jnp.where(odd, lower[:, HALF:], lower[:, :cols])
    momentum_ref[:8, :] = base_ref[:8, :] + upper_own / total_clients
    momentum_ref[8:, :] = base_ref[8:, :] + lower_own / total_clients
    counts = jnp.where(odd, upper[:1, :cohort_count], upper[:1, cols : cols + cohort_count])
    next_ref[...] = log_ref[:, :cohort_count] - 0.2 * (counts / (total_clients // cohort_count) - 0.5)


def per_device(updates, momentum, log_thresholds, cohort_of, seeds, round_index, coef_index):
    local_clients, _, width = updates.shape
    rows, cols = momentum.shape
    cohort_count = log_thresholds.shape[0]
    total_clients = cohort_of.shape[0]
    shards = lax.axis_size("shard")
    chips = lax.axis_size("chip")
    vmem = pl.BlockSpec(memory_space=pltpu.VMEM)
    hbm = pl.BlockSpec(memory_space=pltpu.HBM)
    smem = pl.BlockSpec(memory_space=pltpu.SMEM)
    params = pltpu.CompilerParams(vmem_limit_bytes=24 * MIB)
    row = jax.ShapeDtypeStruct((1, LANES), jnp.float32)

    held, partial, momentum_v, seed_row, log_row, limit, member = pl.pallas_call(
        square_kernel,
        out_shape=(
            pltpu.VMEM(updates.shape, jnp.bfloat16),
            jax.ShapeDtypeStruct((shards, 1, LANES), jnp.float32),
            pltpu.VMEM((rows, cols), jnp.float32),
            jax.ShapeDtypeStruct((1, LANES), jnp.int32),
            row,
            row,
            jax.ShapeDtypeStruct((local_clients, LANES), jnp.float32),
        ),
        in_specs=[hbm] * 5,
        out_specs=(vmem,) * 7,
        scratch_shapes=[
            pltpu.SMEM((cohort_count,), jnp.float32),
            pltpu.SMEM((total_clients,), jnp.int32),
            pltpu.SMEM(seeds.shape, jnp.int32),
            pltpu.VMEM((local_clients, rows, LANES), jnp.float32),
            pltpu.SemaphoreType.DMA((4,)),
            pltpu.SemaphoreType.DMA((local_clients,)),
        ],
        compiler_params=params,
        name="squares",
    )(*(
        pltpu.with_memory_space_constraint(x, pltpu.HBM)
        for x in (log_thresholds, cohort_of, seeds, momentum, updates)
    ))

    squares = lax.all_to_all(partial, "shard", 0, 0, tiled=True)

    def base_of(*refs):
        base_kernel(width, total_clients, seeds.shape[0], *refs)

    base = pl.pallas_call(
        base_of,
        out_shape=jax.ShapeDtypeStruct((rows, cols), jnp.float32),
        in_specs=[smem] * 2 + [vmem] * 3,
        out_specs=vmem,
        compiler_params=params,
        cost_estimate=pl.CostEstimate(
            flops=200 * momentum.size, bytes_accessed=8 * momentum.size, transcendentals=0
        ),
        name="base",
    )(round_index, coef_index, seed_row, log_row, momentum_v)

    def weighted(other):
        def weight(*refs):
            weight_kernel(other, *refs)

        return pl.pallas_call(
            weight,
            out_shape=jax.ShapeDtypeStruct((chips, 8, SLAB), jnp.float32),
            in_specs=[vmem] * 4,
            out_specs=vmem,
            compiler_params=params,
            cost_estimate=pl.CostEstimate(
                flops=2 * updates.size, bytes_accessed=updates.size, transcendentals=0
            ),
            name="weighted_theirs" if other else "weighted_own",
        )(limit, member, squares, held)

    theirs = weighted(1)
    theirs, round_index, coef_index = lax.optimization_barrier((theirs, round_index, coef_index))
    arrived = lax.ppermute(theirs, "core", [(0, 1), (1, 0)])
    own = weighted(0)

    both = pl.pallas_call(
        add_kernel,
        out_shape=pltpu.VMEM(own.shape, jnp.float32),
        in_specs=[vmem] * 2,
        out_specs=vmem,
        compiler_params=params,
        name="add_cores",
    )(own, arrived)
    parts = lax.all_to_all(both, "chip", 0, 0, tiled=True)

    def finish(*refs):
        finish_kernel(total_clients, cohort_count, *refs)

    momentum_next, log_next = pl.pallas_call(
        finish,
        out_shape=(
            jax.ShapeDtypeStruct((rows, cols), jnp.float32),
            jax.ShapeDtypeStruct((1, cohort_count), jnp.float32),
        ),
        in_specs=[vmem] * 3,
        out_specs=(vmem,) * 2,
        compiler_params=params,
        name="finish",
    )(log_row, base, parts)
    return (momentum_next, log_next.reshape(cohort_count))


def solution(mesh):
    clients, shards = mesh.devices.shape
    split = Mesh(mesh.devices.reshape(clients // 2, 2, shards), ("chip", "core", "shard"))
    client = ("chip", "core")
    return jax.shard_map(
        per_device,
        mesh=split,
        in_specs=(P(client, "shard", None), P("shard", client), P(), P(), P(), P(), P()),
        out_specs=(P("shard", client), P()),
        check_vma=False,
    )
```

```python
import jax
import jax.numpy as jnp
from jax import lax
from jax.experimental import pallas as pl
from jax.experimental.pallas import tpu as pltpu
from jax.sharding import Mesh, PartitionSpec as P

LANES = 128
HALF = LANES // 2
MIB = 1024 * 1024

PAIR = 7 * LANES
REACH = 4 * LANES
SLAB = 6 * LANES


def mix(x):
    x = x ^ lax.shift_right_logical(x, jnp.int32(16))
    x = x * jnp.int32(2146121005)
    x = x ^ lax.shift_right_logical(x, jnp.int32(15))
    x = x * jnp.int32(-2073450869)
    x = x ^ lax.shift_right_logical(x, jnp.int32(16))
    return x


def lane_ids(shape):
    return lax.broadcasted_iota(jnp.int32, shape, len(shape) - 1)


def row_ids(shape):
    return lax.broadcasted_iota(jnp.int32, shape, len(shape) - 2)


def diagonal(size):
    return row_ids((size, LANES)) == lane_ids((size, LANES))


def fold(x):
    parts = [x[:, at : at + LANES] for at in range(0, x.shape[1], LANES)]
    while len(parts) > 1:
        parts = [sum(parts[at : at + 2]) for at in range(0, len(parts), 2)]
    return parts[0]


def square_kernel(log_hbm, cohort_hbm, seeds_hbm, momentum_hbm, updates_hbm,
                  held_ref, partial_ref, momentum_ref, seeds_ref, log_ref, limit_ref, member_ref,
                  log_s, cohort_s, seeds_s, sums_v, small_sems, sems):
    local_clients, row_count, width = held_ref.shape
    cohort_count = log_s.shape[0]
    def arrival(c):
        return pltpu.make_async_copy(updates_hbm.at[c], held_ref.at[c], sems.at[c])

    early = 2
    for c in range(early):
        arrival(c).start()
    small = []
    for k, (source, target) in enumerate((
        (log_hbm, log_s), (cohort_hbm, cohort_s), (seeds_hbm, seeds_s), (momentum_hbm, momentum_ref),
    )):
        small.append(pltpu.make_async_copy(source, target, small_sems.at[k]))
        small[-1].start()
    for c in range(early, local_clients):
        arrival(c).start()

    step = 2 * PAIR

    def add_client(c, carry):
        arrival(c).wait()
        acc = jnp.zeros((row_count, step), jnp.float32)
        for at in range(0, width, step):
            block = held_ref[c, :, at : at + step].astype(jnp.float32)
            acc = acc + block * block
        sums_v[c] = fold(acc)
        return carry

    lax.fori_loop(0, early, add_client, 0)
    for copy in small:
        copy.wait()

    lanes = lane_ids((1, LANES))
    own = (2 * lax.axis_index("chip") + lax.axis_index("core")) * local_clients
    logs = jnp.full((1, LANES), log_s[0], jnp.float32)
    for g in range(1, cohort_count):
        logs = jnp.where(lanes == g, log_s[g], logs)
    log_ref[...] = logs
    seed_row = jnp.zeros((1, LANES), jnp.int32)
    for j in range(seeds_s.shape[0]):
        seed_row = jnp.where(lanes == j, seeds_s[j], seed_row)
    seeds_ref[...] = seed_row
    own_logs = jnp.zeros((1, LANES), jnp.float32)
    for c in range(local_clients):
        cohort = cohort_s[own + c]
        own_logs = jnp.where(lanes == c, log_s[cohort], own_logs)
        member_ref[c : c + 1, :] = jnp.where((lanes & (HALF - 1)) == cohort, 1.0, 0.0)
    limit_ref[...] = jnp.exp(own_logs)

    lax.fori_loop(early, local_clients, add_client, 0)
    column = jnp.sum(jnp.sum(sums_v[...], axis=1), axis=1, keepdims=True)
    row = jnp.sum(jnp.where(diagonal(local_clients), column, 0.0), axis=0, keepdims=True)
    partial_ref[...] = jnp.broadcast_to(row[None], partial_ref.shape)


def weight_kernel(other, limit_ref, member_ref, squares_ref, held_ref, _, slab_ref):
    local_clients, row_count, width = held_ref.shape
    odd = (lax.axis_index("core") + other) % 2
    norms = jnp.sqrt(jnp.sum(squares_ref[...], axis=0))
    limit = limit_ref[...]
    factor = limit / jnp.maximum(norms, limit)
    factors = [jnp.broadcast_to(factor[:, c : c + 1], (row_count, REACH)) for c in range(local_clients)]
    bit = (norms <= limit).astype(jnp.float32)
    bits = jnp.sum(jnp.where(diagonal(local_clients), bit, 0.0), axis=1, keepdims=True)
    counts = jnp.sum(member_ref[...] * bits, axis=0, keepdims=True)
    eight = (8, LANES)
    counts = jnp.where(row_ids(eight) == 0, counts, 0.0)
    left = lane_ids(eight) < HALF
    spare_first = left & (odd == 1)
    spare_last = jnp.logical_not(left) & (odd == 0)

    def pair(p, carry):
        at = pl.multiple_of(p * PAIR + odd * (PAIR - REACH), LANES)
        acc = jnp.zeros((row_count, REACH), jnp.float32)
        for c in range(local_clients):
            acc = acc + held_ref[c, :, pl.ds(at, REACH)].astype(jnp.float32) * factors[c]
        upper = [acc[:8, j * LANES : (j + 1) * LANES] for j in range(4)]
        lower = [acc[8:, j * LANES : (j + 1) * LANES] for j in range(4)]
        upper[0] = jnp.where(spare_first, counts, upper[0])
        upper[3] = jnp.where(spare_last, counts, upper[3])
        for j in range(4):
            slab_ref[p, :, j * LANES : (j + 1) * LANES] = upper[j]
        for j in range(2):
            slab_ref[p, :, (4 + j) * LANES : (5 + j) * LANES] = jnp.concatenate(
                [lower[j], lower[j + 2]], axis=0
            )
        return carry

    lax.fori_loop(0, width // PAIR, pair, 0, unroll=4)


def base_kernel(width, total_clients, band, round_s, coef_s, seeds_ref, log_ref, momentum_ref, _, base_ref):
    rows, cols = momentum_ref.shape
    first_row = lax.axis_index("shard") * rows
    first_col = (2 * lax.axis_index("chip") + lax.axis_index("core")) * cols
    block = (rows, cols)
    index = (first_row + row_ids(block)) * jnp.int32(width) + (first_col + lane_ids(block))
    spread = index * jnp.int32(1013904223)
    keys = mix(seeds_ref[...] ^ ((round_s[0] - lane_ids((1, LANES))) * jnp.int32(1640531527)))
    rate = 0.4 + 0.07 * jnp.full((1, 1), coef_s[0], jnp.int32).astype(jnp.float32)
    coef = jnp.ones((1, 1), jnp.float32)
    noise = jnp.zeros(block, jnp.float32)
    for j in range(band):
        if j:
            coef = coef * (rate * ((2.0 * j - 1.0) / (2.0 * j)))
        hashed = mix(spread + keys[:, j : j + 1])
        uniform = (lax.shift_right_logical(hashed, jnp.int32(8)).astype(jnp.float32) + 0.5) * (
            1.0 / 16777216.0
        )
        noise = noise + coef * (3.4641016151377544 * (uniform - 0.5))
    largest = jnp.max(jnp.exp(log_ref[...]), axis=1, keepdims=True)
    base_ref[...] = 0.9 * momentum_ref[...] + (0.05 * largest * noise) / total_clients


def add_kernel(one_ref, other_ref, sum_ref):
    sum_ref[...] = one_ref[...] + other_ref[...]


def finish_kernel(total_clients, cohort_count, log_ref, base_ref, slab_ref, momentum_ref, next_ref):
    cols = base_ref.shape[1]
    odd = lax.axis_index("core") == 1
    total = jnp.sum(slab_ref[...], axis=0)
    upper = total[:, :REACH]
    lower = jnp.concatenate([total[:4, REACH:], total[4:, REACH:]], axis=1)
    upper_own = jnp.where(odd, upper[:, HALF:], upper[:, :cols])
    lower_own = jnp.where(odd, lower[:, HALF:], lower[:, :cols])
    momentum_ref[:8, :] = base_ref[:8, :] + upper_own / total_clients
    momentum_ref[8:, :] = base_ref[8:, :] + lower_own / total_clients
    counts = jnp.where(odd, upper[:1, :cohort_count], upper[:1, cols : cols + cohort_count])
    next_ref[...] = log_ref[:, :cohort_count] - 0.2 * (counts / (total_clients // cohort_count) - 0.5)


def per_device(updates, momentum, log_thresholds, cohort_of, seeds, round_index, coef_index):
    local_clients, _, width = updates.shape
    rows, cols = momentum.shape
    cohort_count = log_thresholds.shape[0]
    total_clients = cohort_of.shape[0]
    shards = lax.axis_size("shard")
    chips = lax.axis_size("chip")
    vmem = pl.BlockSpec(memory_space=pltpu.VMEM)
    hbm = pl.BlockSpec(memory_space=pltpu.HBM)
    smem = pl.BlockSpec(memory_space=pltpu.SMEM)
    anywhere = pl.BlockSpec(memory_space=pl.ANY)
    params = pltpu.CompilerParams(vmem_limit_bytes=24 * MIB)
    row = jax.ShapeDtypeStruct((1, LANES), jnp.float32)

    held, partial, momentum_v, seed_row, log_row, limit, member = pl.pallas_call(
        square_kernel,
        out_shape=(
            pltpu.VMEM(updates.shape, jnp.bfloat16),
            jax.ShapeDtypeStruct((shards, 1, LANES), jnp.float32),
            pltpu.VMEM((rows, cols), jnp.float32),
            jax.ShapeDtypeStruct((1, LANES), jnp.int32),
            row,
            row,
            jax.ShapeDtypeStruct((local_clients, LANES), jnp.float32),
        ),
        in_specs=[hbm] * 5,
        out_specs=(vmem,) * 7,
        scratch_shapes=[
            pltpu.SMEM((cohort_count,), jnp.float32),
            pltpu.SMEM((total_clients,), jnp.int32),
            pltpu.SMEM(seeds.shape, jnp.int32),
            pltpu.VMEM((local_clients, rows, LANES), jnp.float32),
            pltpu.SemaphoreType.DMA((4,)),
            pltpu.SemaphoreType.DMA((local_clients,)),
        ],
        compiler_params=params,
        name="squares",
    )(*(
        pltpu.with_memory_space_constraint(x, pltpu.HBM)
        for x in (log_thresholds, cohort_of, seeds, momentum, updates)
    ))

    squares = lax.all_to_all(partial, "shard", 0, 0, tiled=True)

    def base_of(*refs):
        base_kernel(width, total_clients, seeds.shape[0], *refs)

    base = pl.pallas_call(
        base_of,
        out_shape=jax.ShapeDtypeStruct((rows, cols), jnp.float32),
        in_specs=[smem] * 2 + [vmem] * 3 + [anywhere],
        out_specs=vmem,
        compiler_params=params,
        cost_estimate=pl.CostEstimate(
            flops=200 * momentum.size, bytes_accessed=8 * momentum.size, transcendentals=0
        ),
        name="base",
    )(round_index, coef_index, seed_row, log_row, momentum_v, partial)

    def weighted(other):
        def weight(*refs):
            weight_kernel(other, *refs)

        return pl.pallas_call(
            weight,
            out_shape=jax.ShapeDtypeStruct((chips, 8, SLAB), jnp.float32),
            in_specs=[vmem] * 4 + [anywhere],
            out_specs=vmem,
            compiler_params=params,
            cost_estimate=pl.CostEstimate(
                flops=2 * updates.size, bytes_accessed=updates.size, transcendentals=0
            ),
            name="weighted_theirs" if other else "weighted_own",
        )(limit, member, squares, held, base)

    theirs = weighted(1)
    arrived = lax.ppermute(theirs, "core", [(0, 1), (1, 0)])
    own = weighted(0)

    both = pl.pallas_call(
        add_kernel,
        out_shape=jax.ShapeDtypeStruct(own.shape, jnp.float32),
        in_specs=[vmem] * 2,
        out_specs=vmem,
        compiler_params=params,
        name="add_cores",
    )(own, arrived)
    parts = lax.all_to_all(both, "chip", 0, 0, tiled=True)

    def finish(*refs):
        finish_kernel(total_clients, cohort_count, *refs)

    momentum_next, log_next = pl.pallas_call(
        finish,
        out_shape=(
            jax.ShapeDtypeStruct((rows, cols), jnp.float32),
            jax.ShapeDtypeStruct((1, cohort_count), jnp.float32),
        ),
        in_specs=[vmem] * 3,
        out_specs=(vmem,) * 2,
        compiler_params=params,
        name="finish",
    )(log_row, base, parts)
    return (momentum_next, log_next.reshape(cohort_count))


def solution(mesh):
    clients, shards = mesh.devices.shape
    split = Mesh(mesh.devices.reshape(clients // 2, 2, shards), ("chip", "core", "shard"))
    client = ("chip", "core")
    return jax.shard_map(
        per_device,
        mesh=split,
        in_specs=(P(client, "shard", None), P("shard", client), P(), P(), P(), P(), P()),
        out_specs=(P("shard", client), P()),
        check_vma=False,
    )
```

```python
import math

import jax
import jax.numpy as jnp
from jax import lax
from jax.experimental import pallas as pl
from jax.experimental.pallas import tpu as pltpu
from jax.sharding import Mesh, PartitionSpec as P

LANES = 128
HALF = LANES // 2
MIB = 1024 * 1024

PAIR = 7 * LANES
REACH = 4 * LANES
SLAB = 6 * LANES


def mix(x):
    x = x ^ lax.shift_right_logical(x, jnp.int32(16))
    x = x * jnp.int32(2146121005)
    x = x ^ lax.shift_right_logical(x, jnp.int32(15))
    x = x * jnp.int32(-2073450869)
    x = x ^ lax.shift_right_logical(x, jnp.int32(16))
    return x


def lane_ids(shape):
    return lax.broadcasted_iota(jnp.int32, shape, len(shape) - 1)


def row_ids(shape):
    return lax.broadcasted_iota(jnp.int32, shape, len(shape) - 2)


def diagonal(size):
    return row_ids((size, LANES)) == lane_ids((size, LANES))


def fold(x):
    parts = [x[:, at : at + LANES] for at in range(0, x.shape[1], LANES)]
    while len(parts) > 1:
        parts = [sum(parts[at : at + 2]) for at in range(0, len(parts), 2)]
    return parts[0]


def square_kernel(log_hbm, cohort_hbm, seeds_hbm, momentum_hbm, updates_hbm,
                  held_ref, partial_ref, momentum_ref, seeds_ref, log_ref, limit_ref, member_ref,
                  log_s, cohort_s, seeds_s, sums_v, small_sems, sems):
    local_clients, row_count, width = held_ref.shape
    cohort_count = log_s.shape[0]
    def arrival(c):
        return pltpu.make_async_copy(updates_hbm.at[c], held_ref.at[c], sems.at[c])

    early = 2
    for c in range(early):
        arrival(c).start()
    small = []
    for k, (source, target) in enumerate((
        (log_hbm, log_s), (cohort_hbm, cohort_s), (seeds_hbm, seeds_s), (momentum_hbm, momentum_ref),
    )):
        small.append(pltpu.make_async_copy(source, target, small_sems.at[k]))
        small[-1].start()
    for c in range(early, local_clients):
        arrival(c).start()

    step = 2 * PAIR

    def add_client(c, carry):
        arrival(c).wait()
        acc = jnp.zeros((row_count, step), jnp.float32)
        for at in range(0, width, step):
            block = held_ref[c, :, at : at + step].astype(jnp.float32)
            acc = acc + block * block
        sums_v[c] = fold(acc)
        return carry

    lax.fori_loop(0, early, add_client, 0)
    for copy in small:
        copy.wait()

    lanes = lane_ids((1, LANES))
    own = (2 * lax.axis_index("chip") + lax.axis_index("core")) * local_clients
    logs = jnp.full((1, LANES), log_s[0], jnp.float32)
    for g in range(1, cohort_count):
        logs = jnp.where(lanes == g, log_s[g], logs)
    log_ref[...] = logs
    seed_row = jnp.zeros((1, LANES), jnp.int32)
    for j in range(seeds_s.shape[0]):
        seed_row = jnp.where(lanes == j, seeds_s[j], seed_row)
    seeds_ref[...] = seed_row
    own_logs = jnp.zeros((1, LANES), jnp.float32)
    for c in range(local_clients):
        cohort = cohort_s[own + c]
        own_logs = jnp.where(lanes == c, log_s[cohort], own_logs)
        member_ref[c : c + 1, :] = jnp.where((lanes & (HALF - 1)) == cohort, 1.0, 0.0)
    limit_ref[...] = jnp.exp(own_logs)

    lax.fori_loop(early, local_clients, add_client, 0)
    column = jnp.sum(jnp.sum(sums_v[...], axis=1), axis=1, keepdims=True)
    partial_ref[...] = jnp.sum(jnp.where(diagonal(local_clients), column, 0.0), axis=0, keepdims=True)


def weight_kernel(other, limit_ref, member_ref, squares_ref, held_ref, slab_ref):
    local_clients, row_count, width = held_ref.shape
    odd = (lax.axis_index("core") + other) % 2
    norms = jnp.sqrt(squares_ref[...])
    limit = limit_ref[...]
    factor = limit / jnp.maximum(norms, limit)
    factors = [jnp.broadcast_to(factor[:, c : c + 1], (row_count, REACH)) for c in range(local_clients)]
    bit = (norms <= limit).astype(jnp.float32)
    bits = jnp.sum(jnp.where(diagonal(local_clients), bit, 0.0), axis=1, keepdims=True)
    counts = jnp.sum(member_ref[...] * bits, axis=0, keepdims=True)
    eight = (8, LANES)
    counts = jnp.where(row_ids(eight) == 0, counts, 0.0)
    left = lane_ids(eight) < HALF
    spare_first = left & (odd == 1)
    spare_last = jnp.logical_not(left) & (odd == 0)

    def pair(p, carry):
        at = pl.multiple_of(p * PAIR + odd * (PAIR - REACH), LANES)
        acc = jnp.zeros((row_count, REACH), jnp.float32)
        for c in range(local_clients):
            acc = acc + held_ref[c, :, pl.ds(at, REACH)].astype(jnp.float32) * factors[c]
        upper = [acc[:8, j * LANES : (j + 1) * LANES] for j in range(4)]
        lower = [acc[8:, j * LANES : (j + 1) * LANES] for j in range(4)]
        upper[0] = jnp.where(spare_first, counts, upper[0])
        upper[3] = jnp.where(spare_last, counts, upper[3])
        for j in range(4):
            slab_ref[p, :, j * LANES : (j + 1) * LANES] = upper[j]
        for j in range(2):
            slab_ref[p, :, (4 + j) * LANES : (5 + j) * LANES] = jnp.concatenate(
                [lower[j], lower[j + 2]], axis=0
            )
        return carry

    lax.fori_loop(0, width // PAIR, pair, 0, unroll=4)


def base_kernel(width, total_clients, band, round_s, coef_s, seeds_ref, log_ref, momentum_ref, base_ref):
    rows, cols = momentum_ref.shape
    first_row = lax.axis_index("shard") * rows
    first_col = (2 * lax.axis_index("chip") + lax.axis_index("core")) * cols
    block = (rows, cols)
    index = (first_row + row_ids(block)) * jnp.int32(width) + (first_col + lane_ids(block))
    spread = index * jnp.int32(1013904223)
    keys = mix(seeds_ref[...] ^ ((round_s[0] - lane_ids((1, LANES))) * jnp.int32(1640531527)))
    rate = 0.4 + 0.07 * jnp.full((1, 1), coef_s[0], jnp.int32).astype(jnp.float32)
    coef = jnp.ones((1, 1), jnp.float32)
    noise = jnp.zeros(block, jnp.float32)
    for j in range(band):
        if j:
            coef = coef * (rate * ((2.0 * j - 1.0) / (2.0 * j)))
        hashed = mix(spread + keys[:, j : j + 1])
        uniform = (lax.shift_right_logical(hashed, jnp.int32(8)).astype(jnp.float32) + 0.5) * (
            1.0 / 16777216.0
        )
        noise = noise + coef * (3.4641016151377544 * (uniform - 0.5))
    largest = jnp.max(jnp.exp(log_ref[...]), axis=1, keepdims=True)
    base_ref[...] = 0.9 * momentum_ref[...] + (0.05 * largest * noise) / total_clients


def add_kernel(one_ref, other_ref, sum_ref):
    sum_ref[...] = one_ref[...] + other_ref[...]


def finish_kernel(total_clients, cohort_count, log_ref, base_ref, slab_ref, momentum_ref, next_ref):
    cols = base_ref.shape[1]
    odd = lax.axis_index("core") == 1
    total = jnp.sum(slab_ref[...], axis=0)
    upper = total[:, :REACH]
    lower = jnp.concatenate([total[:4, REACH:], total[4:, REACH:]], axis=1)
    upper_own = jnp.where(odd, upper[:, HALF:], upper[:, :cols])
    lower_own = jnp.where(odd, lower[:, HALF:], lower[:, :cols])
    momentum_ref[:8, :] = base_ref[:8, :] + upper_own / total_clients
    momentum_ref[8:, :] = base_ref[8:, :] + lower_own / total_clients
    counts = jnp.where(odd, upper[:1, :cohort_count], upper[:1, cols : cols + cohort_count])
    next_ref[...] = log_ref[:, :cohort_count] - 0.2 * (counts / (total_clients // cohort_count) - 0.5)


def per_device(updates, momentum, log_thresholds, cohort_of, seeds, round_index, coef_index):
    local_clients, _, width = updates.shape
    rows, cols = momentum.shape
    cohort_count = log_thresholds.shape[0]
    total_clients = cohort_of.shape[0]
    shards = lax.axis_size("shard")
    chips = lax.axis_size("chip")
    vmem = pl.BlockSpec(memory_space=pltpu.VMEM)
    hbm = pl.BlockSpec(memory_space=pltpu.HBM)
    smem = pl.BlockSpec(memory_space=pltpu.SMEM)
    params = pltpu.CompilerParams(vmem_limit_bytes=24 * MIB)
    row = jax.ShapeDtypeStruct((1, LANES), jnp.float32)

    held, partial, momentum_v, seed_row, log_row, limit, member = pl.pallas_call(
        square_kernel,
        out_shape=(
            pltpu.VMEM(updates.shape, jnp.bfloat16),
            row,
            pltpu.VMEM((rows, cols), jnp.float32),
            jax.ShapeDtypeStruct((1, LANES), jnp.int32),
            row,
            row,
            jax.ShapeDtypeStruct((local_clients, LANES), jnp.float32),
        ),
        in_specs=[hbm] * 5,
        out_specs=(vmem,) * 7,
        scratch_shapes=[
            pltpu.SMEM((cohort_count,), jnp.float32),
            pltpu.SMEM((total_clients,), jnp.int32),
            pltpu.SMEM(seeds.shape, jnp.int32),
            pltpu.VMEM((local_clients, rows, LANES), jnp.float32),
            pltpu.SemaphoreType.DMA((4,)),
            pltpu.SemaphoreType.DMA((local_clients,)),
        ],
        compiler_params=params,
        name="squares",
    )(*(
        pltpu.with_memory_space_constraint(x, pltpu.HBM)
        for x in (log_thresholds, cohort_of, seeds, momentum, updates)
    ))

    ring = math.isqrt(shards)
    near = [[ring * i + j for j in range(ring)] for i in range(shards // ring)]
    far = [[ring * i + j for i in range(shards // ring)] for j in range(ring)]
    squares = lax.psum(partial, "shard", axis_index_groups=near)
    squares = lax.psum(squares, "shard", axis_index_groups=far)

    def base_of(*refs):
        base_kernel(width, total_clients, seeds.shape[0], *refs)

    base = pl.pallas_call(
        base_of,
        out_shape=jax.ShapeDtypeStruct((rows, cols), jnp.float32),
        in_specs=[smem] * 2 + [vmem] * 3,
        out_specs=vmem,
        compiler_params=params,
        cost_estimate=pl.CostEstimate(
            flops=200 * momentum.size, bytes_accessed=8 * momentum.size, transcendentals=0
        ),
        name="base",
    )(round_index, coef_index, seed_row, log_row, momentum_v)

    def weighted(other):
        def weight(*refs):
            weight_kernel(other, *refs)

        return pl.pallas_call(
            weight,
            out_shape=jax.ShapeDtypeStruct((chips, 8, SLAB), jnp.float32),
            in_specs=[vmem] * 4,
            out_specs=vmem,
            compiler_params=params,
            cost_estimate=pl.CostEstimate(
                flops=2 * updates.size, bytes_accessed=updates.size, transcendentals=0
            ),
            name="weighted_theirs" if other else "weighted_own",
        )(limit, member, squares, held)

    theirs = weighted(1)
    theirs, round_index, coef_index = lax.optimization_barrier((theirs, round_index, coef_index))
    arrived = lax.ppermute(theirs, "core", [(0, 1), (1, 0)])
    own = weighted(0)

    both = pl.pallas_call(
        add_kernel,
        out_shape=pltpu.VMEM(own.shape, jnp.float32),
        in_specs=[vmem] * 2,
        out_specs=vmem,
        compiler_params=params,
        name="add_cores",
    )(own, arrived)
    parts = lax.all_to_all(both, "chip", 0, 0, tiled=True)

    def finish(*refs):
        finish_kernel(total_clients, cohort_count, *refs)

    momentum_next, log_next = pl.pallas_call(
        finish,
        out_shape=(
            jax.ShapeDtypeStruct((rows, cols), jnp.float32),
            jax.ShapeDtypeStruct((1, cohort_count), jnp.float32),
        ),
        in_specs=[vmem] * 3,
        out_specs=(vmem,) * 2,
        compiler_params=params,
        name="finish",
    )(log_row, base, parts)
    return (momentum_next, log_next.reshape(cohort_count))


def solution(mesh):
    clients, shards = mesh.devices.shape
    split = Mesh(mesh.devices.reshape(clients // 2, 2, shards), ("chip", "core", "shard"))
    client = ("chip", "core")
    return jax.shard_map(
        per_device,
        mesh=split,
        in_specs=(P(client, "shard", None), P("shard", client), P(), P(), P(), P(), P()),
        out_specs=(P("shard", client), P()),
        check_vma=False,
    )
```

```python
import jax
import jax.numpy as jnp
from jax import lax
from jax.experimental import pallas as pl
from jax.experimental.pallas import tpu as pltpu
from jax.sharding import Mesh, PartitionSpec as P

LANES = 128
HALF = LANES // 2
MIB = 1024 * 1024

PAIR = 7 * LANES
REACH = 4 * LANES
SLAB = 6 * LANES


def mix(x):
    x = x ^ lax.shift_right_logical(x, jnp.int32(16))
    x = x * jnp.int32(2146121005)
    x = x ^ lax.shift_right_logical(x, jnp.int32(15))
    x = x * jnp.int32(-2073450869)
    x = x ^ lax.shift_right_logical(x, jnp.int32(16))
    return x


def lane_ids(shape):
    return lax.broadcasted_iota(jnp.int32, shape, len(shape) - 1)


def row_ids(shape):
    return lax.broadcasted_iota(jnp.int32, shape, len(shape) - 2)


def diagonal(size):
    return row_ids((size, LANES)) == lane_ids((size, LANES))


def fold(x):
    parts = [x[:, at : at + LANES] for at in range(0, x.shape[1], LANES)]
    while len(parts) > 1:
        parts = [sum(parts[at : at + 2]) for at in range(0, len(parts), 2)]
    return parts[0]


def square_kernel(log_hbm, cohort_hbm, seeds_hbm, momentum_hbm, updates_hbm,
                  held_ref, partial_ref, momentum_ref, seeds_ref, log_ref, limit_ref, member_ref,
                  log_s, cohort_s, seeds_s, sums_v, small_sems, sems):
    local_clients, row_count, width = held_ref.shape
    cohort_count = log_s.shape[0]
    def arrival(c):
        return pltpu.make_async_copy(updates_hbm.at[c], held_ref.at[c], sems.at[c])

    early, ahead = 2, 6
    for c in range(early):
        arrival(c).start()
    small = []
    for k, (source, target) in enumerate((
        (log_hbm, log_s), (cohort_hbm, cohort_s), (seeds_hbm, seeds_s), (momentum_hbm, momentum_ref),
    )):
        small.append(pltpu.make_async_copy(source, target, small_sems.at[k]))
        small[-1].start()
    for c in range(early, ahead):
        arrival(c).start()

    step = 2 * PAIR

    def add_client(c, follows):
        arrival(c).wait()
        if follows:
            arrival(c + ahead).start()
        acc = jnp.zeros((row_count, step), jnp.float32)
        for at in range(0, width, step):
            block = held_ref[c, :, at : at + step].astype(jnp.float32)
            acc = acc + block * block
        sums_v[c] = jnp.sum(fold(acc), axis=0, keepdims=True)

    def add_clients(first, last, follows):
        def step(c, carry):
            add_client(c, follows)
            return carry

        lax.fori_loop(first, last, step, 0)

    add_clients(0, early, True)
    for copy in small:
        copy.wait()

    lanes = lane_ids((1, LANES))
    own = (2 * lax.axis_index("chip") + lax.axis_index("core")) * local_clients
    logs = jnp.full((1, LANES), log_s[0], jnp.float32)
    for g in range(1, cohort_count):
        logs = jnp.where(lanes == g, log_s[g], logs)
    log_ref[...] = logs
    seed_row = jnp.zeros((1, LANES), jnp.int32)
    for j in range(seeds_s.shape[0]):
        seed_row = jnp.where(lanes == j, seeds_s[j], seed_row)
    seeds_ref[...] = seed_row
    own_logs = jnp.zeros((1, LANES), jnp.float32)
    for c in range(local_clients):
        cohort = cohort_s[own + c]
        own_logs = jnp.where(lanes == c, log_s[cohort], own_logs)
        member_ref[c : c + 1, :] = jnp.where((lanes & (HALF - 1)) == cohort, 1.0, 0.0)
    limit_ref[...] = jnp.exp(own_logs)

    add_clients(early, local_clients - ahead, True)
    add_clients(local_clients - ahead, local_clients, False)
    column = jnp.sum(sums_v[...][:, 0, :], axis=1, keepdims=True)
    row = jnp.sum(jnp.where(diagonal(local_clients), column, 0.0), axis=0, keepdims=True)
    partial_ref[...] = jnp.broadcast_to(row[None], partial_ref.shape)


def weight_kernel(other, limit_ref, member_ref, squares_ref, held_ref, slab_ref):
    local_clients, row_count, width = held_ref.shape
    odd = (lax.axis_index("core") + other) % 2
    norms = jnp.sqrt(jnp.sum(squares_ref[...], axis=0))
    limit = limit_ref[...]
    factor = limit / jnp.maximum(norms, limit)
    factors = [jnp.broadcast_to(factor[:, c : c + 1], (row_count, REACH)) for c in range(local_clients)]
    bit = (norms <= limit).astype(jnp.float32)
    bits = jnp.sum(jnp.where(diagonal(local_clients), bit, 0.0), axis=1, keepdims=True)
    counts = jnp.sum(member_ref[...] * bits, axis=0, keepdims=True)
    eight = (8, LANES)
    counts = jnp.where(row_ids(eight) == 0, counts, 0.0)
    left = lane_ids(eight) < HALF
    spare_first = left & (odd == 1)
    spare_last = jnp.logical_not(left) & (odd == 0)

    def pair(p, carry):
        at = pl.multiple_of(p * PAIR + odd * (PAIR - REACH), LANES)
        acc = jnp.zeros((row_count, REACH), jnp.float32)
        for c in range(local_clients):
            acc = acc + held_ref[c, :, pl.ds(at, REACH)].astype(jnp.float32) * factors[c]
        upper = [acc[:8, j * LANES : (j + 1) * LANES] for j in range(4)]
        lower = [acc[8:, j * LANES : (j + 1) * LANES] for j in range(4)]
        upper[0] = jnp.where(spare_first, counts, upper[0])
        upper[3] = jnp.where(spare_last, counts, upper[3])
        for j in range(4):
            slab_ref[p, :, j * LANES : (j + 1) * LANES] = upper[j]
        for j in range(2):
            slab_ref[p, :, (4 + j) * LANES : (5 + j) * LANES] = jnp.concatenate(
                [lower[j], lower[j + 2]], axis=0
            )
        return carry

    lax.fori_loop(0, width // PAIR, pair, 0, unroll=4)


def base_kernel(width, total_clients, band, round_s, coef_s, seeds_ref, log_ref, momentum_ref, base_ref):
    rows, cols = momentum_ref.shape
    first_row = lax.axis_index("shard") * rows
    first_col = (2 * lax.axis_index("chip") + lax.axis_index("core")) * cols
    block = (rows, cols)
    index = (first_row + row_ids(block)) * jnp.int32(width) + (first_col + lane_ids(block))
    spread = index * jnp.int32(1013904223)
    keys = mix(seeds_ref[...] ^ ((round_s[0] - lane_ids((1, LANES))) * jnp.int32(1640531527)))
    rate = 0.4 + 0.07 * jnp.full((1, 1), coef_s[0], jnp.int32).astype(jnp.float32)
    coef = jnp.ones((1, 1), jnp.float32)
    noise = jnp.zeros(block, jnp.float32)
    for j in range(band):
        if j:
            coef = coef * (rate * ((2.0 * j - 1.0) / (2.0 * j)))
        hashed = mix(spread + keys[:, j : j + 1])
        uniform = (lax.shift_right_logical(hashed, jnp.int32(8)).astype(jnp.float32) + 0.5) * (
            1.0 / 16777216.0
        )
        noise = noise + coef * (3.4641016151377544 * (uniform - 0.5))
    largest = jnp.max(jnp.exp(log_ref[...]), axis=1, keepdims=True)
    base_ref[...] = 0.9 * momentum_ref[...] + (0.05 * largest * noise) / total_clients


def add_kernel(one_ref, other_ref, sum_ref):
    sum_ref[...] = one_ref[...] + other_ref[...]


def finish_kernel(total_clients, cohort_count, log_ref, base_ref, slab_ref, momentum_ref, next_ref):
    cols = base_ref.shape[1]
    odd = lax.axis_index("core") == 1
    total = jnp.sum(slab_ref[...], axis=0)
    upper = total[:, :REACH]
    lower = jnp.concatenate([total[:4, REACH:], total[4:, REACH:]], axis=1)
    upper_own = jnp.where(odd, upper[:, HALF:], upper[:, :cols])
    lower_own = jnp.where(odd, lower[:, HALF:], lower[:, :cols])
    momentum_ref[:8, :] = base_ref[:8, :] + upper_own / total_clients
    momentum_ref[8:, :] = base_ref[8:, :] + lower_own / total_clients
    counts = jnp.where(odd, upper[:1, :cohort_count], upper[:1, cols : cols + cohort_count])
    next_ref[...] = log_ref[:, :cohort_count] - 0.2 * (counts / (total_clients // cohort_count) - 0.5)


def per_device(updates, momentum, log_thresholds, cohort_of, seeds, round_index, coef_index):
    local_clients, _, width = updates.shape
    rows, cols = momentum.shape
    cohort_count = log_thresholds.shape[0]
    total_clients = cohort_of.shape[0]
    shards = lax.axis_size("shard")
    chips = lax.axis_size("chip")
    vmem = pl.BlockSpec(memory_space=pltpu.VMEM)
    hbm = pl.BlockSpec(memory_space=pltpu.HBM)
    smem = pl.BlockSpec(memory_space=pltpu.SMEM)
    params = pltpu.CompilerParams(vmem_limit_bytes=24 * MIB)
    row = jax.ShapeDtypeStruct((1, LANES), jnp.float32)

    held, partial, momentum_v, seed_row, log_row, limit, member = pl.pallas_call(
        square_kernel,
        out_shape=(
            pltpu.VMEM(updates.shape, jnp.bfloat16),
            jax.ShapeDtypeStruct((shards, 1, LANES), jnp.float32),
            pltpu.VMEM((rows, cols), jnp.float32),
            jax.ShapeDtypeStruct((1, LANES), jnp.int32),
            row,
            row,
            jax.ShapeDtypeStruct((local_clients, LANES), jnp.float32),
        ),
        in_specs=[hbm] * 5,
        out_specs=(vmem,) * 7,
        scratch_shapes=[
            pltpu.SMEM((cohort_count,), jnp.float32),
            pltpu.SMEM((total_clients,), jnp.int32),
            pltpu.SMEM(seeds.shape, jnp.int32),
            pltpu.VMEM((local_clients, 1, LANES), jnp.float32),
            pltpu.SemaphoreType.DMA((4,)),
            pltpu.SemaphoreType.DMA((local_clients,)),
        ],
        compiler_params=params,
        name="squares",
    )(*(
        pltpu.with_memory_space_constraint(x, pltpu.HBM)
        for x in (log_thresholds, cohort_of, seeds, momentum, updates)
    ))

    partial, round_index, coef_index = lax.optimization_barrier((partial, round_index, coef_index))
    squares = lax.all_to_all(
        partial, "shard", 0, 0, tiled=True, axis_index_groups=[list(range(shards))]
    )

    def base_of(*refs):
        base_kernel(width, total_clients, seeds.shape[0], *refs)

    base = pl.pallas_call(
        base_of,
        out_shape=jax.ShapeDtypeStruct((rows, cols), jnp.float32),
        in_specs=[smem] * 2 + [vmem] * 3,
        out_specs=vmem,
        compiler_params=params,
        cost_estimate=pl.CostEstimate(
            flops=200 * momentum.size, bytes_accessed=8 * momentum.size, transcendentals=0
        ),
        name="base",
    )(round_index, coef_index, seed_row, log_row, momentum_v)

    def weighted(other):
        def weight(*refs):
            weight_kernel(other, *refs)

        return pl.pallas_call(
            weight,
            out_shape=jax.ShapeDtypeStruct((chips, 8, SLAB), jnp.float32),
            in_specs=[vmem] * 4,
            out_specs=vmem,
            compiler_params=params,
            cost_estimate=pl.CostEstimate(
                flops=2 * updates.size, bytes_accessed=updates.size, transcendentals=0
            ),
            name="weighted_theirs" if other else "weighted_own",
        )(limit, member, squares, held)

    theirs = weighted(1)
    arrived = lax.ppermute(theirs, "core", [(0, 1), (1, 0)])
    own = weighted(0)

    both = pl.pallas_call(
        add_kernel,
        out_shape=jax.ShapeDtypeStruct(own.shape, jnp.float32),
        in_specs=[vmem] * 2,
        out_specs=vmem,
        compiler_params=params,
        name="add_cores",
    )(own, arrived)
    both, base = lax.optimization_barrier((both, base))
    parts = lax.all_to_all(both, "chip", 0, 0, tiled=True)

    def finish(*refs):
        finish_kernel(total_clients, cohort_count, *refs)

    momentum_next, log_next = pl.pallas_call(
        finish,
        out_shape=(
            jax.ShapeDtypeStruct((rows, cols), jnp.float32),
            jax.ShapeDtypeStruct((1, cohort_count), jnp.float32),
        ),
        in_specs=[vmem] * 3,
        out_specs=(vmem,) * 2,
        compiler_params=params,
        name="finish",
    )(log_row, base, parts)
    return (momentum_next, log_next.reshape(cohort_count))


def solution(mesh):
    clients, shards = mesh.devices.shape
    split = Mesh(mesh.devices.reshape(clients // 2, 2, shards), ("chip", "core", "shard"))
    client = ("chip", "core")
    return jax.shard_map(
        per_device,
        mesh=split,
        in_specs=(P(client, "shard", None), P("shard", client), P(), P(), P(), P(), P()),
        out_specs=(P("shard", client), P()),
        check_vma=False,
    )
```

```python
import jax
import jax.numpy as jnp
from jax import lax
from jax.experimental import pallas as pl
from jax.experimental.pallas import tpu as pltpu
from jax.sharding import Mesh, PartitionSpec as P

LANES = 128
HALF = LANES // 2
MIB = 1024 * 1024

PAIR = 7 * LANES
REACH = 4 * LANES
SLAB = 6 * LANES


def mix(x):
    x = x ^ lax.shift_right_logical(x, jnp.int32(16))
    x = x * jnp.int32(2146121005)
    x = x ^ lax.shift_right_logical(x, jnp.int32(15))
    x = x * jnp.int32(-2073450869)
    x = x ^ lax.shift_right_logical(x, jnp.int32(16))
    return x


def lane_ids(shape):
    return lax.broadcasted_iota(jnp.int32, shape, len(shape) - 1)


def row_ids(shape):
    return lax.broadcasted_iota(jnp.int32, shape, len(shape) - 2)


def diagonal(size):
    return row_ids((size, LANES)) == lane_ids((size, LANES))


def fold(x):
    parts = [x[:, at : at + LANES] for at in range(0, x.shape[1], LANES)]
    while len(parts) > 1:
        parts = [sum(parts[at : at + 2]) for at in range(0, len(parts), 2)]
    return parts[0]


def square_kernel(log_hbm, cohort_hbm, seeds_hbm, momentum_hbm, updates_hbm,
                  held_ref, partial_ref, momentum_ref, seeds_ref, log_ref, limit_ref, member_ref,
                  log_s, cohort_s, seeds_s, sums_v, small_sems, sems):
    local_clients, row_count, width = held_ref.shape
    cohort_count = log_s.shape[0]
    ends = [0, 4, 8, 11, 12]
    copies = [
        pltpu.make_async_copy(
            updates_hbm.at[first:last], held_ref.at[first:last], sems.at[k]
        ) for k, (first, last) in enumerate(zip(ends, ends[1:]))
    ]
    copies[0].start()
    small = []
    for k, (source, target) in enumerate((
        (log_hbm, log_s), (cohort_hbm, cohort_s), (seeds_hbm, seeds_s), (momentum_hbm, momentum_ref),
    )):
        small.append(pltpu.make_async_copy(source, target, small_sems.at[k]))
        small[-1].start()
    for copy in copies[1:]:
        copy.start()

    step = 2 * PAIR

    def add_client(c, carry):
        acc = jnp.zeros((row_count, step), jnp.float32)
        for at in range(0, width, step):
            block = held_ref[c, :, at : at + step].astype(jnp.float32)
            acc = acc + block * block
        sums_v[c] = jnp.sum(fold(acc), axis=0, keepdims=True)
        return carry

    def add_clients(k):
        copies[k].wait()
        lax.fori_loop(ends[k], ends[k + 1], add_client, 0)

    add_clients(0)
    for copy in small:
        copy.wait()

    lanes = lane_ids((1, LANES))
    own = (2 * lax.axis_index("chip") + lax.axis_index("core")) * local_clients
    logs = jnp.full((1, LANES), log_s[0], jnp.float32)
    for g in range(1, cohort_count):
        logs = jnp.where(lanes == g, log_s[g], logs)
    log_ref[...] = logs
    seed_row = jnp.zeros((1, LANES), jnp.int32)
    for j in range(seeds_s.shape[0]):
        seed_row = jnp.where(lanes == j, seeds_s[j], seed_row)
    seeds_ref[...] = seed_row
    own_logs = jnp.zeros((1, LANES), jnp.float32)
    for c in range(local_clients):
        cohort = cohort_s[own + c]
        own_logs = jnp.where(lanes == c, log_s[cohort], own_logs)
        member_ref[c : c + 1, :] = jnp.where((lanes & (HALF - 1)) == cohort, 1.0, 0.0)
    limit_ref[...] = jnp.exp(own_logs)

    for k in range(1, len(copies)):
        add_clients(k)
    column = jnp.sum(sums_v[...][:, 0, :], axis=1, keepdims=True)
    row = jnp.sum(jnp.where(diagonal(local_clients), column, 0.0), axis=0, keepdims=True)
    partial_ref[...] = jnp.broadcast_to(row[None], partial_ref.shape)


def write_slabs(odd, factors, counts, held_ref, slab_ref):
    local_clients, row_count, width = held_ref.shape
    left = lane_ids((8, LANES)) < HALF
    spare_first = left & (odd == 1)
    spare_last = jnp.logical_not(left) & (odd == 0)

    def pair(p, carry):
        at = pl.multiple_of(p * PAIR + odd * (PAIR - REACH), LANES)
        acc = jnp.zeros((row_count, REACH), jnp.float32)
        for c in range(local_clients):
            acc = acc + held_ref[c, :, pl.ds(at, REACH)].astype(jnp.float32) * factors[c]
        upper = [acc[:8, j * LANES : (j + 1) * LANES] for j in range(4)]
        lower = [acc[8:, j * LANES : (j + 1) * LANES] for j in range(4)]
        upper[0] = jnp.where(spare_first, counts, upper[0])
        upper[3] = jnp.where(spare_last, counts, upper[3])
        for j in range(4):
            slab_ref[p, :, j * LANES : (j + 1) * LANES] = upper[j]
        for j in range(2):
            slab_ref[p, :, (4 + j) * LANES : (5 + j) * LANES] = jnp.concatenate(
                [lower[j], lower[j + 2]], axis=0
            )
        return carry

    lax.fori_loop(0, width // PAIR, pair, 0, unroll=4)


def theirs_kernel(limit_ref, member_ref, squares_ref, held_ref, slab_ref, factors_ref, counts_ref):
    local_clients, row_count, _ = held_ref.shape
    norms = jnp.sqrt(jnp.sum(squares_ref[...], axis=0))
    limit = limit_ref[...]
    factor = limit / jnp.maximum(norms, limit)
    factors = [jnp.broadcast_to(factor[:, c : c + 1], (row_count, REACH)) for c in range(local_clients)]
    for c in range(local_clients):
        factors_ref[c : c + 1, :] = factors[c][:1, :LANES]
    bit = (norms <= limit).astype(jnp.float32)
    bits = jnp.sum(jnp.where(diagonal(local_clients), bit, 0.0), axis=1, keepdims=True)
    counts = jnp.sum(member_ref[...] * bits, axis=0, keepdims=True)
    counts = jnp.where(row_ids((8, LANES)) == 0, counts, 0.0)
    counts_ref[...] = counts
    write_slabs(1 - lax.axis_index("core"), factors, counts, held_ref, slab_ref)


def own_kernel(width, total_clients, band, round_s, coef_s, seeds_ref, log_ref, momentum_ref,
               factors_ref, counts_ref, held_ref, slab_ref, base_ref):
    write_base(width, total_clients, band, round_s, coef_s, seeds_ref, log_ref, momentum_ref, base_ref)
    local_clients, row_count, _ = held_ref.shape
    factors = [
        jnp.concatenate(
            [jnp.broadcast_to(factors_ref[c : c + 1, :], (row_count, LANES))] * (REACH // LANES), axis=1
        ) for c in range(local_clients)
    ]
    write_slabs(lax.axis_index("core"), factors, counts_ref[...], held_ref, slab_ref)


def write_base(width, total_clients, band, round_s, coef_s, seeds_ref, log_ref, momentum_ref, base_ref):
    rows, cols = momentum_ref.shape
    first_row = lax.axis_index("shard") * rows
    first_col = (2 * lax.axis_index("chip") + lax.axis_index("core")) * cols
    block = (rows, cols)
    index = (first_row + row_ids(block)) * jnp.int32(width) + (first_col + lane_ids(block))
    spread = index * jnp.int32(1013904223)
    keys = mix(seeds_ref[...] ^ ((round_s[0] - lane_ids((1, LANES))) * jnp.int32(1640531527)))
    rate = 0.4 + 0.07 * jnp.full((1, 1), coef_s[0], jnp.int32).astype(jnp.float32)
    coef = jnp.ones((1, 1), jnp.float32)
    noise = jnp.zeros(block, jnp.float32)
    for j in range(band):
        if j:
            coef = coef * (rate * ((2.0 * j - 1.0) / (2.0 * j)))
        hashed = mix(spread + keys[:, j : j + 1])
        uniform = (lax.shift_right_logical(hashed, jnp.int32(8)).astype(jnp.float32) + 0.5) * (
            1.0 / 16777216.0
        )
        noise = noise + coef * (3.4641016151377544 * (uniform - 0.5))
    largest = jnp.max(jnp.exp(log_ref[...]), axis=1, keepdims=True)
    base_ref[...] = 0.9 * momentum_ref[...] + (0.05 * largest * noise) / total_clients


def add_kernel(one_ref, other_ref, sum_ref):
    sum_ref[...] = one_ref[...] + other_ref[...]


def finish_kernel(total_clients, cohort_count, log_ref, base_ref, slab_ref, momentum_ref, next_ref):
    cols = base_ref.shape[1]
    odd = lax.axis_index("core") == 1
    total = jnp.sum(slab_ref[...], axis=0)
    upper = total[:, :REACH]
    lower = jnp.concatenate([total[:4, REACH:], total[4:, REACH:]], axis=1)
    upper_own = jnp.where(odd, upper[:, HALF:], upper[:, :cols])
    lower_own = jnp.where(odd, lower[:, HALF:], lower[:, :cols])
    momentum_ref[:8, :] = base_ref[:8, :] + upper_own / total_clients
    momentum_ref[8:, :] = base_ref[8:, :] + lower_own / total_clients
    counts = jnp.where(odd, upper[:1, :cohort_count], upper[:1, cols : cols + cohort_count])
    next_ref[...] = log_ref[:, :cohort_count] - 0.2 * (counts / (total_clients // cohort_count) - 0.5)


def per_device(updates, momentum, log_thresholds, cohort_of, seeds, round_index, coef_index):
    local_clients, _, width = updates.shape
    rows, cols = momentum.shape
    cohort_count = log_thresholds.shape[0]
    total_clients = cohort_of.shape[0]
    shards = lax.axis_size("shard")
    chips = lax.axis_size("chip")
    vmem = pl.BlockSpec(memory_space=pltpu.VMEM)
    hbm = pl.BlockSpec(memory_space=pltpu.HBM)
    smem = pl.BlockSpec(memory_space=pltpu.SMEM)
    params = pltpu.CompilerParams(vmem_limit_bytes=24 * MIB)
    row = jax.ShapeDtypeStruct((1, LANES), jnp.float32)

    held, partial, momentum_v, seed_row, log_row, limit, member = pl.pallas_call(
        square_kernel,
        out_shape=(
            pltpu.VMEM(updates.shape, jnp.bfloat16),
            jax.ShapeDtypeStruct((shards, 1, LANES), jnp.float32),
            pltpu.VMEM((rows, cols), jnp.float32),
            jax.ShapeDtypeStruct((1, LANES), jnp.int32),
            row,
            row,
            jax.ShapeDtypeStruct((local_clients, LANES), jnp.float32),
        ),
        in_specs=[hbm] * 5,
        out_specs=(vmem,) * 7,
        scratch_shapes=[
            pltpu.SMEM((cohort_count,), jnp.float32),
            pltpu.SMEM((total_clients,), jnp.int32),
            pltpu.SMEM(seeds.shape, jnp.int32),
            pltpu.VMEM((local_clients, 1, LANES), jnp.float32),
            pltpu.SemaphoreType.DMA((4,)),
            pltpu.SemaphoreType.DMA((4,)),
        ],
        compiler_params=params,
        name="squares",
    )(*(
        pltpu.with_memory_space_constraint(x, pltpu.HBM)
        for x in (log_thresholds, cohort_of, seeds, momentum, updates)
    ))

    partial, round_index, coef_index = lax.optimization_barrier((partial, round_index, coef_index))
    squares = lax.all_to_all(
        partial, "shard", 0, 0, tiled=True, axis_index_groups=[list(range(shards))]
    )

    slabs = jax.ShapeDtypeStruct((chips, 8, SLAB), jnp.float32)
    theirs, factors, counts = pl.pallas_call(
        theirs_kernel,
        out_shape=(
            slabs,
            jax.ShapeDtypeStruct((local_clients, LANES), jnp.float32),
            jax.ShapeDtypeStruct((8, LANES), jnp.float32),
        ),
        in_specs=[vmem] * 4,
        out_specs=(vmem,) * 3,
        compiler_params=params,
        name="weighted_theirs",
    )(limit, member, squares, held)
    arrived = lax.ppermute(theirs, "core", [(0, 1), (1, 0)])

    def own_of(*refs):
        own_kernel(width, total_clients, seeds.shape[0], *refs)

    own, base = pl.pallas_call(
        own_of,
        out_shape=(slabs, jax.ShapeDtypeStruct((rows, cols), jnp.float32)),
        in_specs=[smem] * 2 + [vmem] * 6,
        out_specs=(vmem,) * 2,
        compiler_params=params,
        cost_estimate=pl.CostEstimate(
            flops=2 * updates.size, bytes_accessed=updates.size, transcendentals=0
        ),
        name="weighted_own",
    )(round_index, coef_index, seed_row, log_row, momentum_v, factors, counts, held)

    both = pl.pallas_call(
        add_kernel,
        out_shape=jax.ShapeDtypeStruct(own.shape, jnp.float32),
        in_specs=[vmem] * 2,
        out_specs=vmem,
        compiler_params=params,
        name="add_cores",
    )(own, arrived)
    parts = lax.all_to_all(both, "chip", 0, 0, tiled=True)

    def finish(*refs):
        finish_kernel(total_clients, cohort_count, *refs)

    momentum_next, log_next = pl.pallas_call(
        finish,
        out_shape=(
            jax.ShapeDtypeStruct((rows, cols), jnp.float32),
            jax.ShapeDtypeStruct((1, cohort_count), jnp.float32),
        ),
        in_specs=[vmem] * 3,
        out_specs=(vmem,) * 2,
        compiler_params=params,
        name="finish",
    )(log_row, base, parts)
    return (momentum_next, log_next.reshape(cohort_count))


def solution(mesh):
    clients, shards = mesh.devices.shape
    split = Mesh(mesh.devices.reshape(clients // 2, 2, shards), ("chip", "core", "shard"))
    client = ("chip", "core")
    return jax.shard_map(
        per_device,
        mesh=split,
        in_specs=(P(client, "shard", None), P("shard", client), P(), P(), P(), P(), P()),
        out_specs=(P("shard", client), P()),
        check_vma=False,
    )
```

```python
import jax
import jax.numpy as jnp
from jax import lax
from jax.experimental import pallas as pl
from jax.experimental.pallas import tpu as pltpu
from jax.sharding import Mesh, PartitionSpec as P

LANES = 128
HALF = LANES // 2
MIB = 1024 * 1024

PAIR = 7 * LANES
REACH = 4 * LANES
SLAB = 6 * LANES


def mix(x):
    x = x ^ lax.shift_right_logical(x, jnp.int32(16))
    x = x * jnp.int32(2146121005)
    x = x ^ lax.shift_right_logical(x, jnp.int32(15))
    x = x * jnp.int32(-2073450869)
    x = x ^ lax.shift_right_logical(x, jnp.int32(16))
    return x


def lane_ids(shape):
    return lax.broadcasted_iota(jnp.int32, shape, len(shape) - 1)


def row_ids(shape):
    return lax.broadcasted_iota(jnp.int32, shape, len(shape) - 2)


def diagonal(size):
    return row_ids((size, LANES)) == lane_ids((size, LANES))


def fold(x):
    parts = [x[:, at : at + LANES] for at in range(0, x.shape[1], LANES)]
    while len(parts) > 1:
        parts = [sum(parts[at : at + 2]) for at in range(0, len(parts), 2)]
    return parts[0]


def square_kernel(log_hbm, cohort_hbm, seeds_hbm, momentum_hbm, updates_hbm,
                  held_ref, partial_ref, momentum_ref, seeds_ref, log_ref, limit_ref, member_ref,
                  log_s, cohort_s, seeds_s, sums_v, small_sems, sems):
    local_clients, row_count, width = held_ref.shape
    cohort_count = log_s.shape[0]
    ends = [0, 6, 11, 12]
    copies = [
        pltpu.make_async_copy(
            updates_hbm.at[first:last], held_ref.at[first:last], sems.at[k]
        ) for k, (first, last) in enumerate(zip(ends, ends[1:]))
    ]
    copies[0].start()
    small = []
    for k, (source, target) in enumerate((
        (log_hbm, log_s), (cohort_hbm, cohort_s), (seeds_hbm, seeds_s), (momentum_hbm, momentum_ref),
    )):
        small.append(pltpu.make_async_copy(source, target, small_sems.at[k]))
        small[-1].start()
    for copy in copies[1:]:
        copy.start()

    step = 2 * PAIR

    def add_client(c, carry):
        acc = jnp.zeros((row_count, step), jnp.float32)
        for at in range(0, width, step):
            block = held_ref[c, :, at : at + step].astype(jnp.float32)
            acc = acc + block * block
        sums_v[c] = jnp.sum(fold(acc), axis=0, keepdims=True)
        return carry

    def add_clients(k):
        copies[k].wait()
        lax.fori_loop(ends[k], ends[k + 1], add_client, 0)

    add_clients(0)
    for copy in small:
        copy.wait()

    lanes = lane_ids((1, LANES))
    own = (2 * lax.axis_index("chip") + lax.axis_index("core")) * local_clients
    logs = jnp.full((1, LANES), log_s[0], jnp.float32)
    for g in range(1, cohort_count):
        logs = jnp.where(lanes == g, log_s[g], logs)
    log_ref[...] = logs
    seed_row = jnp.zeros((1, LANES), jnp.int32)
    for j in range(seeds_s.shape[0]):
        seed_row = jnp.where(lanes == j, seeds_s[j], seed_row)
    seeds_ref[...] = seed_row
    own_logs = jnp.zeros((1, LANES), jnp.float32)
    for c in range(local_clients):
        cohort = cohort_s[own + c]
        own_logs = jnp.where(lanes == c, log_s[cohort], own_logs)
        member_ref[c : c + 1, :] = jnp.where((lanes & (HALF - 1)) == cohort, 1.0, 0.0)
    limit_ref[...] = jnp.exp(own_logs)

    for k in range(1, len(copies)):
        add_clients(k)
    column = jnp.sum(sums_v[...][:, 0, :], axis=1, keepdims=True)
    row = jnp.sum(jnp.where(diagonal(local_clients), column, 0.0), axis=0, keepdims=True)
    partial_ref[...] = jnp.broadcast_to(row[None], partial_ref.shape)


def write_slabs(odd, factors, counts, held_ref, slab_ref):
    local_clients, row_count, width = held_ref.shape
    left = lane_ids((8, LANES)) < HALF
    spare_first = left & (odd == 1)
    spare_last = jnp.logical_not(left) & (odd == 0)

    def pair(p, carry):
        at = pl.multiple_of(p * PAIR + odd * (PAIR - REACH), LANES)
        acc = jnp.zeros((row_count, REACH), jnp.float32)
        for c in range(local_clients):
            acc = acc + held_ref[c, :, pl.ds(at, REACH)].astype(jnp.float32) * factors[c]
        upper = [acc[:8, j * LANES : (j + 1) * LANES] for j in range(4)]
        lower = [acc[8:, j * LANES : (j + 1) * LANES] for j in range(4)]
        upper[0] = jnp.where(spare_first, counts, upper[0])
        upper[3] = jnp.where(spare_last, counts, upper[3])
        for j in range(4):
            slab_ref[p, :, j * LANES : (j + 1) * LANES] = upper[j]
        for j in range(2):
            slab_ref[p, :, (4 + j) * LANES : (5 + j) * LANES] = jnp.concatenate(
                [lower[j], lower[j + 2]], axis=0
            )
        return carry

    lax.fori_loop(0, width // PAIR, pair, 0, unroll=4)


def theirs_kernel(limit_ref, member_ref, squares_ref, held_ref, slab_ref, factors_ref, counts_ref):
    local_clients, row_count, _ = held_ref.shape
    norms = jnp.sqrt(jnp.sum(squares_ref[...], axis=0))
    limit = limit_ref[...]
    factor = limit / jnp.maximum(norms, limit)
    factors = [jnp.broadcast_to(factor[:, c : c + 1], (row_count, REACH)) for c in range(local_clients)]
    for c in range(local_clients):
        factors_ref[c : c + 1, :] = factors[c][:1, :LANES]
    bit = (norms <= limit).astype(jnp.float32)
    bits = jnp.sum(jnp.where(diagonal(local_clients), bit, 0.0), axis=1, keepdims=True)
    counts = jnp.sum(member_ref[...] * bits, axis=0, keepdims=True)
    counts = jnp.where(row_ids((8, LANES)) == 0, counts, 0.0)
    counts_ref[...] = counts
    write_slabs(1 - lax.axis_index("core"), factors, counts, held_ref, slab_ref)


def own_kernel(width, total_clients, band, round_s, coef_s, seeds_ref, log_ref, momentum_ref,
               factors_ref, counts_ref, held_ref, slab_ref, base_ref):
    write_base(width, total_clients, band, round_s, coef_s, seeds_ref, log_ref, momentum_ref, base_ref)
    local_clients, row_count, _ = held_ref.shape
    factors = [
        jnp.concatenate(
            [jnp.broadcast_to(factors_ref[c : c + 1, :], (row_count, LANES))] * (REACH // LANES), axis=1
        ) for c in range(local_clients)
    ]
    write_slabs(lax.axis_index("core"), factors, counts_ref[...], held_ref, slab_ref)


def write_base(width, total_clients, band, round_s, coef_s, seeds_ref, log_ref, momentum_ref, base_ref):
    rows, cols = momentum_ref.shape
    first_row = lax.axis_index("shard") * rows
    first_col = (2 * lax.axis_index("chip") + lax.axis_index("core")) * cols
    block = (rows, cols)
    index = (first_row + row_ids(block)) * jnp.int32(width) + (first_col + lane_ids(block))
    spread = index * jnp.int32(1013904223)
    keys = mix(seeds_ref[...] ^ ((round_s[0] - lane_ids((1, LANES))) * jnp.int32(1640531527)))
    rate = 0.4 + 0.07 * jnp.full((1, 1), coef_s[0], jnp.int32).astype(jnp.float32)
    coef = jnp.ones((1, 1), jnp.float32)
    noise = jnp.zeros(block, jnp.float32)
    for j in range(band):
        if j:
            coef = coef * (rate * ((2.0 * j - 1.0) / (2.0 * j)))
        hashed = mix(spread + keys[:, j : j + 1])
        uniform = (lax.shift_right_logical(hashed, jnp.int32(8)).astype(jnp.float32) + 0.5) * (
            1.0 / 16777216.0
        )
        noise = noise + coef * (3.4641016151377544 * (uniform - 0.5))
    largest = jnp.max(jnp.exp(log_ref[...]), axis=1, keepdims=True)
    base_ref[...] = 0.9 * momentum_ref[...] + (0.05 * largest * noise) / total_clients


def add_kernel(one_ref, other_ref, sum_ref):
    sum_ref[...] = one_ref[...] + other_ref[...]


def finish_kernel(total_clients, cohort_count, log_ref, base_ref, slab_ref, momentum_ref, next_ref):
    cols = base_ref.shape[1]
    odd = lax.axis_index("core") == 1
    parts = [slab_ref[k] for k in range(slab_ref.shape[0])]
    while len(parts) > 1:
        parts = [sum(parts[at : at + 2]) for at in range(0, len(parts), 2)]
    total = parts[0]
    share = 1.0 / total_clients
    upper = total[:, :REACH]
    lower = jnp.concatenate([total[:4, REACH:], total[4:, REACH:]], axis=1)
    upper_own = jnp.where(odd, upper[:, HALF:], upper[:, :cols])
    lower_own = jnp.where(odd, lower[:, HALF:], lower[:, :cols])
    momentum_ref[:8, :] = base_ref[:8, :] + upper_own * share
    momentum_ref[8:, :] = base_ref[8:, :] + lower_own * share
    counts = jnp.where(odd, upper[:1, :cohort_count], upper[:1, cols : cols + cohort_count])
    next_ref[...] = log_ref[:, :cohort_count] - 0.2 * (counts / (total_clients // cohort_count) - 0.5)


def per_device(updates, momentum, log_thresholds, cohort_of, seeds, round_index, coef_index):
    local_clients, _, width = updates.shape
    rows, cols = momentum.shape
    cohort_count = log_thresholds.shape[0]
    total_clients = cohort_of.shape[0]
    shards = lax.axis_size("shard")
    chips = lax.axis_size("chip")
    vmem = pl.BlockSpec(memory_space=pltpu.VMEM)
    hbm = pl.BlockSpec(memory_space=pltpu.HBM)
    smem = pl.BlockSpec(memory_space=pltpu.SMEM)
    params = pltpu.CompilerParams(vmem_limit_bytes=24 * MIB)
    row = jax.ShapeDtypeStruct((1, LANES), jnp.float32)

    held, partial, momentum_v, seed_row, log_row, limit, member = pl.pallas_call(
        square_kernel,
        out_shape=(
            pltpu.VMEM(updates.shape, jnp.bfloat16),
            jax.ShapeDtypeStruct((shards, 1, LANES), jnp.float32),
            pltpu.VMEM((rows, cols), jnp.float32),
            jax.ShapeDtypeStruct((1, LANES), jnp.int32),
            row,
            row,
            jax.ShapeDtypeStruct((local_clients, LANES), jnp.float32),
        ),
        in_specs=[hbm] * 5,
        out_specs=(vmem,) * 7,
        scratch_shapes=[
            pltpu.SMEM((cohort_count,), jnp.float32),
            pltpu.SMEM((total_clients,), jnp.int32),
            pltpu.SMEM(seeds.shape, jnp.int32),
            pltpu.VMEM((local_clients, 1, LANES), jnp.float32),
            pltpu.SemaphoreType.DMA((4,)),
            pltpu.SemaphoreType.DMA((3,)),
        ],
        compiler_params=params,
        name="squares",
    )(*(
        pltpu.with_memory_space_constraint(x, pltpu.HBM)
        for x in (log_thresholds, cohort_of, seeds, momentum, updates)
    ))

    partial, round_index, coef_index = lax.optimization_barrier((partial, round_index, coef_index))
    squares = lax.all_to_all(
        partial, "shard", 0, 0, tiled=True, axis_index_groups=[list(range(shards))]
    )

    slabs = jax.ShapeDtypeStruct((chips, 8, SLAB), jnp.float32)
    theirs, factors, counts = pl.pallas_call(
        theirs_kernel,
        out_shape=(
            slabs,
            jax.ShapeDtypeStruct((local_clients, LANES), jnp.float32),
            jax.ShapeDtypeStruct((8, LANES), jnp.float32),
        ),
        in_specs=[vmem] * 4,
        out_specs=(vmem,) * 3,
        compiler_params=params,
        name="weighted_theirs",
    )(limit, member, squares, held)
    arrived = lax.ppermute(theirs, "core", [(0, 1), (1, 0)])

    def own_of(*refs):
        own_kernel(width, total_clients, seeds.shape[0], *refs)

    own, base = pl.pallas_call(
        own_of,
        out_shape=(slabs, jax.ShapeDtypeStruct((rows, cols), jnp.float32)),
        in_specs=[smem] * 2 + [vmem] * 6,
        out_specs=(vmem,) * 2,
        compiler_params=params,
        cost_estimate=pl.CostEstimate(
            flops=2 * updates.size, bytes_accessed=updates.size, transcendentals=0
        ),
        name="weighted_own",
    )(round_index, coef_index, seed_row, log_row, momentum_v, factors, counts, held)

    both = pl.pallas_call(
        add_kernel,
        out_shape=jax.ShapeDtypeStruct(own.shape, jnp.float32),
        in_specs=[vmem] * 2,
        out_specs=vmem,
        compiler_params=params,
        name="add_cores",
    )(own, arrived)
    parts = lax.all_to_all(both, "chip", 0, 0, tiled=True)

    def finish(*refs):
        finish_kernel(total_clients, cohort_count, *refs)

    momentum_next, log_next = pl.pallas_call(
        finish,
        out_shape=(
            jax.ShapeDtypeStruct((rows, cols), jnp.float32),
            jax.ShapeDtypeStruct((1, cohort_count), jnp.float32),
        ),
        in_specs=[vmem] * 3,
        out_specs=(vmem,) * 2,
        compiler_params=params,
        name="finish",
    )(log_row, base, parts)
    return (momentum_next, log_next.reshape(cohort_count))


def solution(mesh):
    clients, shards = mesh.devices.shape
    split = Mesh(mesh.devices.reshape(clients // 2, 2, shards), ("chip", "core", "shard"))
    client = ("chip", "core")
    return jax.shard_map(
        per_device,
        mesh=split,
        in_specs=(P(client, "shard", None), P("shard", client), P(), P(), P(), P(), P()),
        out_specs=(P("shard", client), P()),
        check_vma=False,
    )
```

```python
import jax
import jax.numpy as jnp
from jax import lax
from jax.experimental import pallas as pl
from jax.experimental.pallas import tpu as pltpu
from jax.sharding import Mesh, PartitionSpec as P

LANES = 128
HALF = LANES // 2
MIB = 1024 * 1024

PAIR = 7 * LANES
REACH = 4 * LANES
SLAB = 6 * LANES


def mix(x):
    x = x ^ lax.shift_right_logical(x, jnp.int32(16))
    x = x * jnp.int32(2146121005)
    x = x ^ lax.shift_right_logical(x, jnp.int32(15))
    x = x * jnp.int32(-2073450869)
    x = x ^ lax.shift_right_logical(x, jnp.int32(16))
    return x


def lane_ids(shape):
    return lax.broadcasted_iota(jnp.int32, shape, len(shape) - 1)


def row_ids(shape):
    return lax.broadcasted_iota(jnp.int32, shape, len(shape) - 2)


def diagonal(size):
    return row_ids((size, LANES)) == lane_ids((size, LANES))


def fold(x):
    parts = [x[:, at : at + LANES] for at in range(0, x.shape[1], LANES)]
    while len(parts) > 1:
        parts = [sum(parts[at : at + 2]) for at in range(0, len(parts), 2)]
    return parts[0]


def square_kernel(log_hbm, cohort_hbm, seeds_hbm, momentum_hbm, updates_hbm,
                  held_ref, partial_ref, momentum_ref, seeds_ref, log_ref, limit_ref, member_ref,
                  log_s, cohort_s, seeds_s, sums_v, small_sems, sems):
    local_clients, row_count, width = held_ref.shape
    cohort_count = log_s.shape[0]
    ends = [0, 6, 11, 12]
    copies = [
        pltpu.make_async_copy(
            updates_hbm.at[first:last], held_ref.at[first:last], sems.at[k]
        ) for k, (first, last) in enumerate(zip(ends, ends[1:]))
    ]
    copies[0].start()
    small = []
    for k, (source, target) in enumerate((
        (log_hbm, log_s), (cohort_hbm, cohort_s), (seeds_hbm, seeds_s), (momentum_hbm, momentum_ref),
    )):
        small.append(pltpu.make_async_copy(source, target, small_sems.at[k]))
        small[-1].start()
    for copy in copies[1:]:
        copy.start()

    step = 2 * PAIR

    def add_client(c, carry):
        acc = jnp.zeros((row_count, step), jnp.float32)
        for at in range(0, width, step):
            block = held_ref[c, :, at : at + step].astype(jnp.float32)
            acc = acc + block * block
        sums_v[c] = jnp.sum(fold(acc), axis=0, keepdims=True)
        return carry

    def add_clients(k):
        copies[k].wait()
        lax.fori_loop(ends[k], ends[k + 1], add_client, 0)

    add_clients(0)
    for copy in small:
        copy.wait()

    lanes = lane_ids((1, LANES))
    own = (2 * lax.axis_index("chip") + lax.axis_index("core")) * local_clients
    logs = jnp.full((1, LANES), log_s[0], jnp.float32)
    for g in range(1, cohort_count):
        logs = jnp.where(lanes == g, log_s[g], logs)
    log_ref[...] = logs
    seed_row = jnp.zeros((1, LANES), jnp.int32)
    for j in range(seeds_s.shape[0]):
        seed_row = jnp.where(lanes == j, seeds_s[j], seed_row)
    seeds_ref[...] = seed_row
    own_logs = jnp.zeros((1, LANES), jnp.float32)
    for c in range(local_clients):
        cohort = cohort_s[own + c]
        own_logs = jnp.where(lanes == c, log_s[cohort], own_logs)
        member_ref[c : c + 1, :] = jnp.where((lanes & (HALF - 1)) == cohort, 1.0, 0.0)
    limit_ref[...] = jnp.exp(own_logs)

    for k in range(1, len(copies)):
        add_clients(k)
    column = jnp.sum(sums_v[...][:, 0, :], axis=1, keepdims=True)
    row = jnp.sum(jnp.where(diagonal(local_clients), column, 0.0), axis=0, keepdims=True)
    partial_ref[...] = jnp.broadcast_to(row[None], partial_ref.shape)


def write_slabs(odd, factors, counts, held_ref, slab_ref):
    local_clients, row_count, width = held_ref.shape
    left = lane_ids((8, LANES)) < HALF
    spare_first = left & (odd == 1)
    spare_last = jnp.logical_not(left) & (odd == 0)

    def pair(p, carry):
        at = pl.multiple_of(p * PAIR + odd * (PAIR - REACH), LANES)
        acc = jnp.zeros((row_count, REACH), jnp.float32)
        for c in range(local_clients):
            acc = acc + held_ref[c, :, pl.ds(at, REACH)].astype(jnp.float32) * factors[c]
        upper = [acc[:8, j * LANES : (j + 1) * LANES] for j in range(4)]
        lower = [acc[8:, j * LANES : (j + 1) * LANES] for j in range(4)]
        upper[0] = jnp.where(spare_first, counts, upper[0])
        upper[3] = jnp.where(spare_last, counts, upper[3])
        for j in range(4):
            slab_ref[p, :, j * LANES : (j + 1) * LANES] = upper[j]
        for j in range(2):
            slab_ref[p, :, (4 + j) * LANES : (5 + j) * LANES] = jnp.concatenate(
                [lower[j], lower[j + 2]], axis=0
            )
        return carry

    lax.fori_loop(0, width // PAIR, pair, 0, unroll=8)


def theirs_kernel(limit_ref, member_ref, squares_ref, held_ref, slab_ref, factors_ref, counts_ref):
    local_clients, row_count, _ = held_ref.shape
    norms = jnp.sqrt(jnp.sum(squares_ref[...], axis=0))
    limit = limit_ref[...]
    factor = limit / jnp.maximum(norms, limit)
    factors = [jnp.broadcast_to(factor[:, c : c + 1], (row_count, REACH)) for c in range(local_clients)]
    for c in range(local_clients):
        factors_ref[c : c + 1, :] = factors[c][:1, :LANES]
    bit = (norms <= limit).astype(jnp.float32)
    bits = jnp.sum(jnp.where(diagonal(local_clients), bit, 0.0), axis=1, keepdims=True)
    counts = jnp.sum(member_ref[...] * bits, axis=0, keepdims=True)
    counts = jnp.where(row_ids((8, LANES)) == 0, counts, 0.0)
    counts_ref[...] = counts
    write_slabs(1 - lax.axis_index("core"), factors, counts, held_ref, slab_ref)


def own_kernel(width, total_clients, band, round_s, coef_s, seeds_ref, log_ref, momentum_ref,
               factors_ref, counts_ref, held_ref, slab_ref, base_ref):
    write_base(width, total_clients, band, round_s, coef_s, seeds_ref, log_ref, momentum_ref, base_ref)
    local_clients, row_count, _ = held_ref.shape
    factors = [
        jnp.concatenate(
            [jnp.broadcast_to(factors_ref[c : c + 1, :], (row_count, LANES))] * (REACH // LANES), axis=1
        ) for c in range(local_clients)
    ]
    write_slabs(lax.axis_index("core"), factors, counts_ref[...], held_ref, slab_ref)


def write_base(width, total_clients, band, round_s, coef_s, seeds_ref, log_ref, momentum_ref, base_ref):
    rows, cols = momentum_ref.shape
    first_row = lax.axis_index("shard") * rows
    first_col = (2 * lax.axis_index("chip") + lax.axis_index("core")) * cols
    block = (rows, cols)
    index = (first_row + row_ids(block)) * jnp.int32(width) + (first_col + lane_ids(block))
    spread = index * jnp.int32(1013904223)
    keys = mix(seeds_ref[...] ^ ((round_s[0] - lane_ids((1, LANES))) * jnp.int32(1640531527)))
    rate = 0.4 + 0.07 * jnp.full((1, 1), coef_s[0], jnp.int32).astype(jnp.float32)
    coef = jnp.ones((1, 1), jnp.float32)
    noise = jnp.zeros(block, jnp.float32)
    for j in range(band):
        if j:
            coef = coef * (rate * ((2.0 * j - 1.0) / (2.0 * j)))
        hashed = mix(spread + keys[:, j : j + 1])
        uniform = (lax.shift_right_logical(hashed, jnp.int32(8)).astype(jnp.float32) + 0.5) * (
            1.0 / 16777216.0
        )
        noise = noise + coef * (3.4641016151377544 * (uniform - 0.5))
    largest = jnp.max(jnp.exp(log_ref[...]), axis=1, keepdims=True)
    base_ref[...] = 0.9 * momentum_ref[...] + (0.05 * largest * noise) / total_clients


def add_kernel(one_ref, other_ref, sum_ref):
    sum_ref[...] = one_ref[...] + other_ref[...]


def finish_kernel(total_clients, cohort_count, log_ref, base_ref, slab_ref, momentum_ref, next_ref):
    cols = base_ref.shape[1]
    odd = lax.axis_index("core") == 1
    parts = [slab_ref[k] for k in range(slab_ref.shape[0])]
    while len(parts) > 1:
        parts = [sum(parts[at : at + 2]) for at in range(0, len(parts), 2)]
    total = parts[0]
    share = 1.0 / total_clients
    upper = total[:, :REACH]
    lower = jnp.concatenate([total[:4, REACH:], total[4:, REACH:]], axis=1)
    upper_own = jnp.where(odd, upper[:, HALF:], upper[:, :cols])
    lower_own = jnp.where(odd, lower[:, HALF:], lower[:, :cols])
    momentum_ref[:8, :] = base_ref[:8, :] + upper_own * share
    momentum_ref[8:, :] = base_ref[8:, :] + lower_own * share
    counts = jnp.where(odd, upper[:1, :cohort_count], upper[:1, cols : cols + cohort_count])
    next_ref[...] = log_ref[:, :cohort_count] - 0.2 * (counts / (total_clients // cohort_count) - 0.5)


def per_device(updates, momentum, log_thresholds, cohort_of, seeds, round_index, coef_index):
    local_clients, _, width = updates.shape
    rows, cols = momentum.shape
    cohort_count = log_thresholds.shape[0]
    total_clients = cohort_of.shape[0]
    shards = lax.axis_size("shard")
    chips = lax.axis_size("chip")
    vmem = pl.BlockSpec(memory_space=pltpu.VMEM)
    hbm = pl.BlockSpec(memory_space=pltpu.HBM)
    smem = pl.BlockSpec(memory_space=pltpu.SMEM)
    params = pltpu.CompilerParams(vmem_limit_bytes=24 * MIB)
    row = jax.ShapeDtypeStruct((1, LANES), jnp.float32)

    held, partial, momentum_v, seed_row, log_row, limit, member = pl.pallas_call(
        square_kernel,
        out_shape=(
            pltpu.VMEM(updates.shape, jnp.bfloat16),
            jax.ShapeDtypeStruct((shards, 1, LANES), jnp.float32),
            pltpu.VMEM((rows, cols), jnp.float32),
            jax.ShapeDtypeStruct((1, LANES), jnp.int32),
            row,
            row,
            jax.ShapeDtypeStruct((local_clients, LANES), jnp.float32),
        ),
        in_specs=[hbm] * 5,
        out_specs=(vmem,) * 7,
        scratch_shapes=[
            pltpu.SMEM((cohort_count,), jnp.float32),
            pltpu.SMEM((total_clients,), jnp.int32),
            pltpu.SMEM(seeds.shape, jnp.int32),
            pltpu.VMEM((local_clients, 1, LANES), jnp.float32),
            pltpu.SemaphoreType.DMA((4,)),
            pltpu.SemaphoreType.DMA((3,)),
        ],
        compiler_params=params,
        name="squares",
    )(*(
        pltpu.with_memory_space_constraint(x, pltpu.HBM)
        for x in (log_thresholds, cohort_of, seeds, momentum, updates)
    ))

    partial, round_index, coef_index = lax.optimization_barrier((partial, round_index, coef_index))
    squares = lax.all_to_all(
        partial, "shard", 0, 0, tiled=True, axis_index_groups=[list(range(shards))]
    )

    slabs = jax.ShapeDtypeStruct((chips, 8, SLAB), jnp.float32)
    theirs, factors, counts = pl.pallas_call(
        theirs_kernel,
        out_shape=(
            slabs,
            jax.ShapeDtypeStruct((local_clients, LANES), jnp.float32),
            jax.ShapeDtypeStruct((8, LANES), jnp.float32),
        ),
        in_specs=[vmem] * 4,
        out_specs=(vmem,) * 3,
        compiler_params=params,
        name="weighted_theirs",
    )(limit, member, squares, held)
    arrived = lax.ppermute(theirs, "core", [(0, 1), (1, 0)])

    def own_of(*refs):
        own_kernel(width, total_clients, seeds.shape[0], *refs)

    own, base = pl.pallas_call(
        own_of,
        out_shape=(slabs, jax.ShapeDtypeStruct((rows, cols), jnp.float32)),
        in_specs=[smem] * 2 + [vmem] * 6,
        out_specs=(vmem,) * 2,
        compiler_params=params,
        cost_estimate=pl.CostEstimate(
            flops=2 * updates.size, bytes_accessed=updates.size, transcendentals=0
        ),
        name="weighted_own",
    )(round_index, coef_index, seed_row, log_row, momentum_v, factors, counts, held)

    both = pl.pallas_call(
        add_kernel,
        out_shape=jax.ShapeDtypeStruct(own.shape, jnp.float32),
        in_specs=[vmem] * 2,
        out_specs=vmem,
        compiler_params=params,
        name="add_cores",
    )(own, arrived)
    parts = lax.all_to_all(both, "chip", 0, 0, tiled=True)

    def finish(*refs):
        finish_kernel(total_clients, cohort_count, *refs)

    momentum_next, log_next = pl.pallas_call(
        finish,
        out_shape=(
            jax.ShapeDtypeStruct((rows, cols), jnp.float32),
            jax.ShapeDtypeStruct((1, cohort_count), jnp.float32),
        ),
        in_specs=[vmem] * 3,
        out_specs=(vmem,) * 2,
        compiler_params=params,
        name="finish",
    )(log_row, base, parts)
    return (momentum_next, log_next.reshape(cohort_count))


def solution(mesh):
    clients, shards = mesh.devices.shape
    split = Mesh(mesh.devices.reshape(clients // 2, 2, shards), ("chip", "core", "shard"))
    client = ("chip", "core")
    return jax.shard_map(
        per_device,
        mesh=split,
        in_specs=(P(client, "shard", None), P("shard", client), P(), P(), P(), P(), P()),
        out_specs=(P("shard", client), P()),
        check_vma=False,
    )
```
